128 devices in a mesh: dp: 8 (over z_hi, x), seq: 8 (over z_lo, y), mp: 2 (over core).
Axes of the slice: x: 4, y: 4, z: 4 (z_hi: 2, z_lo: 2; z = z_hi * 2 + z_lo), core: 2. Of those that a mesh axis runs over, the one named last changes fastest.
Arguments:
- queries: bfloat16 [8, 4096, 4096], P('dp', 'seq', 'mp'), may hold values from -140 to 140
- features: bfloat16 [8, 1024, 7680], P(None, ('seq', 'dp')), may hold values from -12 to 12
- w_key: bfloat16 [7680, 512], P(None, 'mp'), may hold values from -0.0625 to 0.0625
- w_value: bfloat16 [7680, 512], P(None, 'mp'), may hold values from -0.0625 to 0.0625
- key_gain: float32 [128], replicated, may hold values from 0.25 to 1.75
- out_grad: bfloat16 [8, 4096, 4096], P('dp', 'seq', 'mp'), may hold values from -6 to 6
- tile_counts: int32 [8], P('dp'), may hold values from 1 to 4, as said below
- text_start: int32 [8], P('dp'), may hold values from 0 to 2048, as said below
Outputs:
- attended: bfloat16 [8, 4096, 4096], P('dp', 'seq', 'mp')
- query_grad: bfloat16 [8, 4096, 4096], P('dp', 'seq', 'mp')
- key_weight_grad: float32 [7680, 512], P(('dp', 'seq'), 'mp')
- value_weight_grad: float32 [7680, 512], P(('dp', 'seq'), 'mp')
The draws below stay inside these ranges and needn't reach their ends.
Inputs may be any that keep to these rules, and one draw needn't show every extreme that they name: Image positions of row b from tile_counts[b] * 256 on are padding that no query sees. Text positions of row b below text_start[b] come before the row's image: they attend to nothing, their output and gradients are zero.
All inputs are finite; a program needn't handle non-finite values.
Results may differ from the reference program's by a relative error of at most 0.035.
The reference program's roundings to bfloat16 on the way count: a program that leaves them out, or rounds other values in their place, can miss the bound.
Values may be sent and summed in bfloat16 or wider, within the bound.
No kernel may reach another device: no remote copies, remote signals or barrier semaphores. Data moves between devices by JAX's collectives and lax.ppermute only.
A program may use at most 128 MiB of HBM per device.

```python
import jax
import jax.numpy as jnp
from jax import lax

FEAT = 7680
HEADS = 32
KV_HEADS = 4
HEAD_DIM = 128
TILES = 4
ROWS = 8
TEXT = 4096
IMG = 1024


def draw_queries(key, part):
    key = jax.random.fold_in(key, 11)
    noise_key = jax.random.fold_in(key, 0)
    values = 2.5 * jax.random.truncated_normal(noise_key, -6.0, 6.0, (ROWS, TEXT, HEADS, HEAD_DIM), jnp.float32)
    return values.reshape(ROWS, TEXT, HEADS * HEAD_DIM).astype(jnp.bfloat16)


def draw_features(key, part):
    key = jax.random.fold_in(key, 23)
    noise_key = jax.random.fold_in(key, 0)
    values = jax.random.truncated_normal(noise_key, -6.0, 6.0, (ROWS, IMG, FEAT), jnp.float32)
    return values.astype(jnp.bfloat16)


def draw_tile_counts(key, part):
    key = jax.random.fold_in(key, 37)
    count_key, first_key, second_key = jax.random.split(key, 3)
    counts = jax.random.randint(count_key, (ROWS,), 1, TILES + 1)
    first_row = jax.random.randint(first_key, (), 0, ROWS)
    second_row = (first_row + 1 + jax.random.randint(second_key, (), 0, ROWS - 1)) % ROWS
    counts = jnp.where(jnp.arange(ROWS) == first_row, TILES, counts)
    counts = jnp.where(jnp.arange(ROWS) == second_row, 1, counts)
    return counts.astype(jnp.int32)


def draw_text_start(key, part):
    key = jax.random.fold_in(key, 41)
    start_key, first_key, second_key = jax.random.split(key, 3)
    starts = jax.random.randint(start_key, (ROWS,), 0, TEXT // 2 + 1)
    first_row = jax.random.randint(first_key, (), 0, ROWS)
    second_row = (first_row + 1 + jax.random.randint(second_key, (), 0, ROWS - 1)) % ROWS
    starts = jnp.where(jnp.arange(ROWS) == first_row, 0, starts)
    starts = jnp.where(jnp.arange(ROWS) == second_row, TEXT // 2, starts)
    return starts.astype(jnp.int32)


def shard_levels(rng, dims, cuts, least, top_value):
    factor_of, own = 1.0, jax.random.fold_in(rng, 6)
    for axis_at, parts in cuts:
        steps = jnp.exp(jax.random.uniform(jax.random.fold_in(own, axis_at), (parts,), jnp.float32, least / len(cuts), top_value / len(cuts)))
        factor_of = factor_of * jnp.repeat(steps, dims[axis_at] // parts).reshape([-1 if axis == axis_at else 1 for axis in range(len(dims))])
    return factor_of


def gaussian(stream_key, shape, scale, reach, shards=(), held_as=jnp.bfloat16):
    drawn = scale * jax.random.normal(stream_key, shape, jnp.float32)
    if shards:
        drawn = drawn * shard_levels(stream_key, shape, shards, -0.22, 0.18)
    return jnp.clip(drawn, -reach, reach).astype(held_as)


def setup_inputs(seed: int = 0) -> dict:
    seeds = jax.random.split(jax.random.key(seed), 9)
    return {
        "queries": draw_queries(jax.random.fold_in(seeds[8], 71), 0),
        "features": draw_features(jax.random.fold_in(seeds[8], 71), 0),
        "w_key": gaussian(seeds[2], (FEAT, KV_HEADS * HEAD_DIM), FEAT ** -0.5, 0.0625, ((1, 2),)),
        "w_value": gaussian(seeds[3], (FEAT, KV_HEADS * HEAD_DIM), FEAT ** -0.5, 0.0625, ((1, 2),)),
        "key_gain": jnp.clip(1.0 + 0.15 * jax.random.normal(seeds[4], (HEAD_DIM,), jnp.float32), 0.25, 1.75),
        "out_grad": gaussian(seeds[5], (ROWS, TEXT, HEADS * HEAD_DIM), 1.0, 6.0, ((0, 8), (1, 8), (2, 2))),
        "tile_counts": draw_tile_counts(jax.random.fold_in(seeds[8], 71), 0),
        "text_start": draw_text_start(jax.random.fold_in(seeds[8], 71), 0),
    }


EPSILON = 1e-05

def normalize_keys(key_pre, key_gain):
    head_rows = key_pre.reshape(key_pre.shape[0], -1, HEAD_DIM)
    factor = lax.rsqrt(lax.optimization_barrier(jnp.mean(head_rows * head_rows, axis=-1, keepdims=True)) + EPSILON)
    return (head_rows, factor, head_rows * factor * key_gain)

def normalize_back(head_rows, factor, key_gain, key_grad):
    gained = key_gain * key_grad
    inner_mean = lax.optimization_barrier(jnp.mean(head_rows * gained, axis=-1, keepdims=True))
    return factor * gained - factor * factor * factor * head_rows * inner_mean

def group_pass(q_group, k_group, v_group, d_group, key_valid, live_rows):
    score_scale = HEAD_DIM ** (-0.5)
    scores = jnp.dot(q_group, k_group.T, preferred_element_type=jnp.float32) * score_scale
    scores = jnp.where(key_valid[None, :], scores, -jnp.inf)
    row_max = lax.optimization_barrier(jnp.max(scores, axis=1, keepdims=True))
    powers = jnp.exp(scores - row_max)
    probabilities = powers / lax.optimization_barrier(jnp.sum(powers, axis=1, keepdims=True))
    prob_rounded = probabilities.astype(jnp.bfloat16)
    output_part = (jnp.dot(prob_rounded, v_group, preferred_element_type=jnp.float32) * live_rows[:, None]).astype(jnp.bfloat16)
    grad_live = d_group * live_rows[:, None].astype(d_group.dtype)
    prob_grad = jnp.dot(grad_live, v_group.T, preferred_element_type=jnp.float32)
    row_delta = lax.optimization_barrier(jnp.sum(probabilities * prob_grad, axis=1, keepdims=True))
    score_grad = (probabilities * (prob_grad - row_delta)).astype(jnp.bfloat16)
    query_part = (jnp.dot(score_grad, k_group, preferred_element_type=jnp.float32) * score_scale).astype(jnp.bfloat16)
    key_part = jnp.dot(score_grad.T, q_group, preferred_element_type=jnp.float32) * score_scale
    value_part = jnp.dot(prob_rounded.T, grad_live, preferred_element_type=jnp.float32)
    return (output_part, query_part, key_part, value_part)

def reference(queries, features, w_key, w_value, key_gain, out_grad, tile_counts, text_start):
    kv_dim = w_key.shape[1]
    groups = kv_dim // HEAD_DIM
    group_size = HEADS // groups
    text_len = queries.shape[1]
    img_len = features.shape[1]

    def regroup(matrix):
        return matrix.reshape(text_len, groups, group_size, HEAD_DIM).transpose(1, 0, 2, 3).reshape(groups, text_len * group_size, HEAD_DIM)

    def ungroup(stacked):
        return stacked.reshape(groups, text_len, group_size * HEAD_DIM).transpose(1, 0, 2).reshape(text_len, HEADS * HEAD_DIM)

    def row_step(running, row_inputs):
        q_row, f_row, d_row, tile_count, start_pos = row_inputs
        key_pre = jnp.dot(f_row, w_key, preferred_element_type=jnp.float32)
        head_rows, factor, normed = normalize_keys(key_pre, key_gain)
        keys = normed.astype(jnp.bfloat16)
        values = jnp.dot(f_row, w_value, preferred_element_type=jnp.float32).astype(jnp.bfloat16).reshape(img_len, groups, HEAD_DIM)
        key_valid = jnp.arange(img_len, dtype=jnp.int32) < tile_count * (img_len // TILES)
        live_mask = (jnp.arange(text_len, dtype=jnp.int32) >= start_pos).astype(jnp.float32)
        live_rows = jnp.repeat(live_mask, group_size)

        def one_group(group_item):
            return group_pass(group_item[0], group_item[1], group_item[2], group_item[3], key_valid, live_rows)
        outputs, query_parts, key_parts, value_parts = lax.map(one_group, (regroup(q_row), keys.transpose(1, 0, 2), values.transpose(1, 0, 2), regroup(d_row)))
        key_grad = key_parts.transpose(1, 0, 2)
        value_grad = value_parts.transpose(1, 0, 2).reshape(img_len, kv_dim)
        pre_grad = normalize_back(head_rows, factor, key_gain, key_grad).reshape(img_len, kv_dim).astype(jnp.bfloat16)
        value_rounded = value_grad.astype(jnp.bfloat16)
        key_total = running[0] + jnp.dot(f_row.T, pre_grad, preferred_element_type=jnp.float32)
        value_total = running[1] + jnp.dot(f_row.T, value_rounded, preferred_element_type=jnp.float32)
        return ((key_total, value_total), (ungroup(outputs), ungroup(query_parts)))
    zero_grad = jnp.zeros((features.shape[2], kv_dim), jnp.float32)
    totals, results = lax.scan(row_step, (zero_grad, zero_grad), (queries, features, out_grad, tile_counts, text_start))
    return (results[0], results[1], totals[0], totals[1])
```

```python
import functools

import jax
import jax.numpy as jnp
from jax import lax
from jax.experimental import pallas as pl
from jax.experimental.pallas import tpu as pltpu
from jax.sharding import PartitionSpec as P

HEAD_DIM = 128
TILES = 4
EPSILON = 1e-05
SCALE = HEAD_DIM**-0.5
EXP2_SCALE = SCALE * 1.4426950408889634
BF16 = jnp.bfloat16
F32 = jnp.float32
LANES = 128
VMEM_LIMIT = 48 * 2**20

NN = (((1,), (0,)), ((), ()))
NT = (((1,), (1,)), ((), ()))


def whole(shape):
    return pl.BlockSpec(shape, lambda *_: (0,) * len(shape))


def params(axes):
    return pltpu.CompilerParams(
        vmem_limit_bytes=VMEM_LIMIT, dimension_semantics=("arbitrary",) * axes
    )


def project_kernel(f_ref, wk_ref, wv_ref, gain_ref, *refs, windows, per_step, groups, copies):
    send_refs, (pre_ref, win_ref, total) = refs[:groups], refs[groups:]
    step, steps = pl.program_id(0), pl.num_programs(0)
    depth = wk_ref.shape[0]
    kv_dim = wk_ref.shape[1]
    width = win_ref.shape[2]
    part = f_ref[:, pl.ds(pl.multiple_of(step * depth, LANES), depth)]

    @pl.when(step == 0)
    def _():
        total[...] = jnp.zeros_like(total)

    total[:, :kv_dim] += jnp.dot(part, wk_ref[...], preferred_element_type=F32)
    total[:, kv_dim:] += jnp.dot(part, wv_ref[...], preferred_element_type=F32)

    @pl.when(step * per_step < windows)
    def _():
        for inner in range(per_step):
            at = step * per_step + inner
            tiles_all = f_ref.shape[1] // LANES
            tile = (at * tiles_all) // windows
            win_ref[inner] = f_ref[:, pl.ds(pl.multiple_of(tile * LANES, LANES), width)]

    @pl.when(step == steps - 1)
    def _():
        pre_ref[...] = total[:, :kv_dim]
        for group in range(groups):
            cols = slice(group * HEAD_DIM, (group + 1) * HEAD_DIM)
            head = total[:, cols]
            factor = lax.rsqrt(jnp.mean(head * head, axis=-1, keepdims=True) + EPSILON)
            key = (head * factor * gain_ref[...]).astype(BF16)
            start = kv_dim + group * HEAD_DIM
            value = total[:, start : start + HEAD_DIM].astype(BF16)
            for copy in range(copies):
                send_refs[group][copy, :, :HEAD_DIM] = key
                send_refs[group][copy, :, HEAD_DIM:] = value


def project(feats, w_key, w_value, gain, windows, copies):
    tokens, feat = feats.shape
    kv_dim = w_key.shape[1]
    groups = kv_dim // HEAD_DIM
    per_step = 2
    steps = windows // per_step + 1
    depth = feat // steps
    width = -(-(feat // windows) // LANES) * LANES
    last = windows // per_step - 1
    sends = [jax.ShapeDtypeStruct((copies, tokens, 2 * HEAD_DIM), BF16)] * groups
    return pl.pallas_call(
        functools.partial(
            project_kernel, windows=windows, per_step=per_step, groups=groups, copies=copies
        ),
        grid=(steps,),
        in_specs=[
            whole((tokens, feat)),
            pl.BlockSpec((depth, kv_dim), lambda k: (k, 0)),
            pl.BlockSpec((depth, kv_dim), lambda k: (k, 0)),
            whole((1, HEAD_DIM)),
        ],
        out_specs=[whole(s.shape) for s in sends]
        + [
            whole((tokens, kv_dim)),
            pl.BlockSpec((per_step, tokens, width), lambda k: (jnp.minimum(k, last), 0, 0)),
        ],
        out_shape=sends
        + [
            jax.ShapeDtypeStruct((tokens, kv_dim), F32),
            jax.ShapeDtypeStruct((windows, tokens, width), BF16),
        ],
        scratch_shapes=[pltpu.VMEM((tokens, 2 * kv_dim), F32)],
        compiler_params=params(1),
        cost_estimate=pl.CostEstimate(
            flops=4 * tokens * feat * kv_dim,
            bytes_accessed=4 * feat * kv_dim + 4 * tokens * feat,
            transcendentals=0,
        ),
        name="project",
    )(feats, w_key, w_value, gain)


def attend_kernel(ctl_ref, q_ref, d_ref, kv_ref, *refs, heads):
    att_ref, dq_ref, dkv_ref, kt_ref, vt_ref, dk_sum, dv_sum = refs[-7:]
    step, steps = pl.program_id(0), pl.num_programs(0)
    rows = q_ref.shape[0]
    img = kv_ref.shape[0]

    @pl.when(step == 0)
    def _():
        dk_sum[...] = jnp.zeros_like(dk_sum)
        dv_sum[...] = jnp.zeros_like(dv_sum)
        kt_ref[...] = kv_ref[:, :HEAD_DIM].T
        vt_ref[...] = kv_ref[:, HEAD_DIM:].T

    def run(length):
        key, value = kv_ref[:length, :HEAD_DIM], kv_ref[:length, HEAD_DIM:]
        key_t, value_t = kt_ref[:, :length], vt_ref[:, :length]
        position = ctl_ref[1] + lax.broadcasted_iota(jnp.int32, (rows, HEAD_DIM), 0)
        live = position >= ctl_ref[2]
        grads, probs, queries, cotangents = [], [], [], []

        def scores_of(head):
            cols = slice(head * HEAD_DIM, (head + 1) * HEAD_DIM)
            query = q_ref[:, cols]
            cotangent = jnp.where(live, d_ref[:, cols], jnp.zeros((), BF16))
            scores = lax.dot_general(key, query, NT, preferred_element_type=F32)
            return cols, query, cotangent, scores

        def finish(cols, query, cotangent, scores):
            row_max = jnp.max(scores, axis=0, keepdims=True)
            powers = jnp.exp2((scores - row_max) * EXP2_SCALE)
            prob = powers * (1.0 / jnp.sum(powers, axis=0, keepdims=True))
            rounded = prob.astype(BF16)
            out_t = lax.dot_general(value_t, rounded, NN, preferred_element_type=F32)
            att_ref[:, cols] = jnp.where(live, out_t.T, 0.0).astype(BF16)
            prob_grad = lax.dot_general(value, cotangent, NT, preferred_element_type=F32)
            delta = jnp.sum(out_t * cotangent.astype(F32).T, axis=0, keepdims=True)
            score_grad = (prob * (prob_grad - delta)).astype(BF16)
            dq_t = lax.dot_general(key_t, score_grad, NN, preferred_element_type=F32)
            dq_ref[:, cols] = (dq_t.T * SCALE).astype(BF16)
            grads.append(score_grad)
            probs.append(rounded)
            queries.append(query)
            cotangents.append(cotangent)

        held = scores_of(0)
        for head in range(heads):
            ahead = scores_of(head + 1) if head + 1 < heads else None
            finish(*held)
            held = ahead
        dk_sum[:length] += jnp.dot(
            jnp.concatenate(grads, axis=1),
            jnp.concatenate(queries, axis=0),
            preferred_element_type=F32,
        )
        dv_sum[:length] += jnp.dot(
            jnp.concatenate(probs, axis=1),
            jnp.concatenate(cotangents, axis=0),
            preferred_element_type=F32,
        )

    for count in range(1, TILES + 1):
        pl.when(ctl_ref[0] == count)(functools.partial(run, count * (img // TILES)))

    @pl.when(step == steps - 1)
    def _():
        dkv_ref[:, :HEAD_DIM] = (dk_sum[...] * SCALE).astype(BF16)
        dkv_ref[:, HEAD_DIM:] = dv_sum[...].astype(BF16)


def attend(ctl, queries, out_grad, keys_values, group, groups, earlier):
    rows, width = queries.shape
    img = keys_values.shape[0]
    heads = 2
    steps = width // groups // HEAD_DIM // heads
    cols = pl.BlockSpec((rows, heads * HEAD_DIM), lambda h, ctl: (0, group * steps + h))
    pair = pl.BlockSpec((img, 2 * HEAD_DIM), lambda h, ctl: (0, 0))
    anywhere = pl.BlockSpec(memory_space=pl.ANY)
    big = jax.ShapeDtypeStruct((rows, width), BF16)
    work = steps * heads * rows * img * HEAD_DIM
    return pl.pallas_call(
        functools.partial(attend_kernel, heads=heads),
        grid_spec=pltpu.PrefetchScalarGridSpec(
            num_scalar_prefetch=1,
            grid=(steps,),
            in_specs=[cols, cols, pair] + [anywhere] * len(earlier),
            out_specs=[cols, cols, pair],
            scratch_shapes=[pltpu.VMEM((HEAD_DIM, img), BF16)] * 2
            + [pltpu.VMEM((img, HEAD_DIM), F32)] * 2,
        ),
        out_shape=[big, big, jax.ShapeDtypeStruct((img, 2 * HEAD_DIM), BF16)],
        input_output_aliases={4 + i: i for i in range(len(earlier))},
        compiler_params=params(1),
        cost_estimate=pl.CostEstimate(
            flops=24 * work, bytes_accessed=8 * rows * width // groups, transcendentals=0
        ),
        name="attend",
    )(ctl, queries, out_grad, keys_values, *earlier)


def norm_back_kernel(parts_ref, pre_ref, gain_ref, out_ref, *, group):
    grad = jnp.sum(parts_ref[...].astype(F32), axis=0)
    head = pre_ref[:, group * HEAD_DIM : (group + 1) * HEAD_DIM]
    factor = lax.rsqrt(jnp.mean(head * head, axis=-1, keepdims=True) + EPSILON)
    gained = gain_ref[...] * grad[:, :HEAD_DIM]
    inner = jnp.mean(head * gained, axis=-1, keepdims=True)
    pre_grad = (factor * gained - factor * factor * factor * head * inner).astype(BF16)
    value_grad = grad[:, HEAD_DIM:].astype(BF16)
    for copy in range(out_ref.shape[0]):
        out_ref[copy, :, :HEAD_DIM] = pre_grad
        out_ref[copy, :, HEAD_DIM:] = value_grad


def norm_back(parts, key_pre, gain, group, copies):
    tokens, width = parts.shape[1:]
    return pl.pallas_call(
        functools.partial(norm_back_kernel, group=group),
        out_shape=jax.ShapeDtypeStruct((copies, tokens, width), BF16),
        compiler_params=pltpu.CompilerParams(vmem_limit_bytes=VMEM_LIMIT),
        name="norm_back",
    )(parts, key_pre, gain)


def turn_kernel(ctl_ref, f_ref, out_ref):
    odd = ctl_ref[3]
    turned = f_ref[...].reshape(-1, f_ref.shape[-1]).T
    rows = out_ref.shape[0]
    spare = turned.shape[0] - rows

    @pl.when(odd == 0)
    def _():
        out_ref[...] = turned[:rows]

    @pl.when(odd != 0)
    def _():
        out_ref[...] = turned[spare:]


def turn(ctl, windows, feat):
    sources, rows, own, width = windows.shape
    tokens = sources * own
    return pl.pallas_call(
        turn_kernel,
        grid_spec=pltpu.PrefetchScalarGridSpec(
            num_scalar_prefetch=1,
            grid=(rows,),
            in_specs=[pl.BlockSpec((sources, 1, own, width), lambda r, ctl: (0, r, 0, 0))],
            out_specs=pl.BlockSpec((feat, tokens), lambda r, ctl: (0, r)),
        ),
        out_shape=jax.ShapeDtypeStruct((feat, rows * tokens), BF16),
        compiler_params=params(1),
        name="turn",
    )(ctl, windows)


def weight_kernel(f_ref, g_ref, out_ref):
    out_ref[...] = jnp.dot(f_ref[...], g_ref[...], preferred_element_type=F32).astype(BF16)


def weight_grad(turned, grads):
    feat, tokens = turned.shape
    width = grads.shape[1]
    return pl.pallas_call(
        weight_kernel,
        out_shape=jax.ShapeDtypeStruct((feat, width), BF16),
        compiler_params=pltpu.CompilerParams(vmem_limit_bytes=VMEM_LIMIT),
        cost_estimate=pl.CostEstimate(
            flops=2 * feat * tokens * width, bytes_accessed=2 * feat * tokens, transcendentals=0
        ),
        name="weight_grad",
    )(turned, grads)


def exchange(array, axes):
    return lax.all_to_all(array, axes, split_axis=0, concat_axis=0, tiled=True)


def on_device(queries, features, w_key, w_value, key_gain, out_grad, tile_counts, text_start):
    dp, seq = lax.axis_size("dp"), lax.axis_size("seq")
    rows, own, feat = features.shape
    text_dev = queries.shape[1]
    kv_dim = w_key.shape[1]
    groups = kv_dim // HEAD_DIM
    tokens = rows * own
    gain = key_gain.reshape(1, HEAD_DIM)
    dp_index, seq_index = lax.axis_index("dp"), lax.axis_index("seq")
    ctl = jnp.stack([tile_counts[0], seq_index * text_dev, text_start[0], dp_index % 2])
    feats = features.reshape(tokens, feat)
    *sends, key_pre, windows = project(feats, w_key, w_value, gain, dp, seq)

    gathered = []
    for send in sends:
        pieces = send.reshape(seq * dp, own, 2 * HEAD_DIM)
        arrived = exchange(pieces, ("seq", "dp"))
        gathered.append(arrived.reshape(seq * tokens, 2 * HEAD_DIM))
    own_pre = exchange(key_pre.reshape(dp, own, kv_dim), "dp").reshape(tokens, kv_dim)
    windows = exchange(windows, "dp").reshape(dp, rows, own, -1)

    earlier = []
    shares = []
    for group in range(groups):
        attended, query_grad, grads = attend(
            ctl, queries[0], out_grad[0], gathered[group], group, groups, earlier
        )
        earlier = [attended, query_grad]
        shares.append(exchange(grads.reshape(seq, tokens, 2 * HEAD_DIM), "seq"))

    turned = turn(ctl, windows, feat // dp)
    key_cols, value_cols = [], []
    for group in range(groups):
        rounded = norm_back(shares[group], own_pre, gain, group, dp)
        everywhere = exchange(rounded, "dp").reshape(dp * tokens, 2 * HEAD_DIM)
        partial = weight_grad(turned, everywhere)
        pieces = exchange(partial.reshape(seq, feat // dp // seq, 2 * HEAD_DIM), "seq")
        summed = jnp.sum(pieces.astype(F32), axis=0)
        key_cols.append(summed[:, :HEAD_DIM])
        value_cols.append(summed[:, HEAD_DIM:])
    return (
        earlier[0][None],
        earlier[1][None],
        jnp.concatenate(key_cols, axis=1),
        jnp.concatenate(value_cols, axis=1),
    )


def solution(mesh):
    placed = (
        P("dp", "seq", "mp"),
        P(None, ("seq", "dp"), None),
        P(None, "mp"),
        P(None, "mp"),
        P(),
        P("dp", "seq", "mp"),
        P("dp"),
        P("dp"),
    )
    return jax.shard_map(
        on_device,
        mesh=mesh,
        in_specs=placed,
        out_specs=(
            P("dp", "seq", "mp"),
            P("dp", "seq", "mp"),
            P(("dp", "seq"), "mp"),
            P(("dp", "seq"), "mp"),
        ),
        check_vma=False,
    )
```

```python
import functools

import jax
import jax.numpy as jnp
from jax import lax
from jax.experimental import pallas as pl
from jax.experimental.pallas import tpu as pltpu
from jax.sharding import PartitionSpec as P

HEAD_DIM = 128
TILES = 4
EPSILON = 1e-05
SCALE = HEAD_DIM**-0.5
EXP2_SCALE = SCALE * 1.4426950408889634
BF16 = jnp.bfloat16
F32 = jnp.float32
LANES = 128
VMEM_LIMIT = 60 * 2**20

NN = (((1,), (0,)), ((), ()))
NT = (((1,), (1,)), ((), ()))


def whole(shape):
    return pl.BlockSpec(shape, lambda *_: (0,) * len(shape))


def params(axes):
    return pltpu.CompilerParams(
        vmem_limit_bytes=VMEM_LIMIT, dimension_semantics=("arbitrary",) * axes
    )


def project_kernel(f_ref, wk_ref, wv_ref, gain_ref, send_ref, win_ref, total):
    step, steps = pl.program_id(0), pl.num_programs(0)
    depth, kv_dim = wk_ref.shape
    windows, tokens, width = win_ref.shape
    tiles = f_ref.shape[1] // LANES
    own = tokens // windows
    part = f_ref[:, pl.ds(pl.multiple_of(step * depth, LANES), depth)]

    @pl.when(step == 0)
    def _():
        total[...] = jnp.zeros_like(total)

    total[:, :kv_dim] += jnp.dot(part, wk_ref[...], preferred_element_type=F32)
    total[:, kv_dim:] += jnp.dot(part, wv_ref[...], preferred_element_type=F32)

    @pl.when(step < windows // 2)
    def _():
        for inner in range(2):
            at = step * 2 + inner
            tile = (at * tiles) // windows
            win_ref[at] = f_ref[:, pl.ds(pl.multiple_of(tile * LANES, LANES), width)]

    @pl.when(step == steps - 1)
    def _():
        for group in range(kv_dim // HEAD_DIM):
            cols = slice(group * HEAD_DIM, (group + 1) * HEAD_DIM)
            head = total[:, cols]
            factor = lax.rsqrt(jnp.mean(head * head, axis=-1, keepdims=True) + EPSILON)
            key = (head * factor * gain_ref[...]).astype(BF16)
            start = kv_dim + group * HEAD_DIM
            value = total[:, start : start + HEAD_DIM].astype(BF16)
            at = 2 * group * HEAD_DIM
            for copy in range(send_ref.shape[0]):
                send_ref[copy, :, at : at + HEAD_DIM] = key
                send_ref[copy, :, at + HEAD_DIM : at + 2 * HEAD_DIM] = value
        lane = lax.broadcasted_iota(jnp.int32, (own, LANES), 1)
        half = LANES // 2
        for window in range(windows):
            head = total[window * own : (window + 1) * own, :kv_dim]
            high = head.astype(BF16).astype(F32)
            pair = jnp.concatenate([high, head - high], axis=1)
            place = 1 - window % 2
            at = (width - LANES) * place
            for block in range(windows):
                piece = pair[:, block // 2 * LANES : (block // 2 + 1) * LANES]
                if block % 2 != place:
                    piece = pltpu.roll(piece, half, axis=1)
                rows = slice(block * own, (block + 1) * own)
                kept = win_ref[window, rows, at : at + LANES].astype(F32)
                mixed = jnp.where((lane >= half) == bool(place), piece, kept)
                win_ref[window, rows, at : at + LANES] = mixed.astype(BF16)


def project(feats, w_key, w_value, gain, windows, copies):
    tokens, feat = feats.shape
    kv_dim = w_key.shape[1]
    steps = windows // 2 + 1
    depth = feat // steps
    width = -(-(feat // windows) // LANES) * LANES
    outs = [(copies, tokens, 2 * kv_dim), (windows, tokens, width)]
    return pl.pallas_call(
        project_kernel,
        grid=(steps,),
        in_specs=[
            whole((tokens, feat)),
            pl.BlockSpec((depth, kv_dim), lambda k: (k, 0)),
            pl.BlockSpec((depth, kv_dim), lambda k: (k, 0)),
            whole((1, HEAD_DIM)),
        ],
        out_specs=[whole(shape) for shape in outs],
        out_shape=[jax.ShapeDtypeStruct(shape, BF16) for shape in outs],
        scratch_shapes=[pltpu.VMEM((tokens, 2 * kv_dim), F32)],
        compiler_params=params(1),
        cost_estimate=pl.CostEstimate(
            flops=4 * tokens * feat * kv_dim,
            bytes_accessed=4 * feat * kv_dim + 4 * tokens * feat,
            transcendentals=0,
        ),
        name="project",
    )(feats, w_key, w_value, gain)


def attend_kernel(
    ctl_ref, q_ref, d_ref, kv_ref, att_ref, dq_ref, dkv_ref, kt_ref, vt_ref, dk_sum, dv_sum, *, heads
):
    step, steps = pl.program_id(1), pl.num_programs(1)
    rows = q_ref.shape[0]
    img = kv_ref.shape[0]

    @pl.when(step == 0)
    def _():
        dk_sum[...] = jnp.zeros_like(dk_sum)
        dv_sum[...] = jnp.zeros_like(dv_sum)
        kt_ref[...] = kv_ref[:, :HEAD_DIM].T
        vt_ref[...] = kv_ref[:, HEAD_DIM:].T

    def run(length):
        key, value = kv_ref[:length, :HEAD_DIM], kv_ref[:length, HEAD_DIM:]
        key_t, value_t = kt_ref[:, :length], vt_ref[:, :length]
        position = ctl_ref[1] + lax.broadcasted_iota(jnp.int32, (rows, HEAD_DIM), 0)
        live = position >= ctl_ref[2]
        grads, probs, queries, cotangents = [], [], [], []

        def scores_of(head):
            cols = slice(head * HEAD_DIM, (head + 1) * HEAD_DIM)
            query = q_ref[:, cols]
            cotangent = jnp.where(live, d_ref[:, cols], jnp.zeros((), BF16))
            scores = lax.dot_general(key, query, NT, preferred_element_type=F32)
            return cols, query, cotangent, scores

        def finish(cols, query, cotangent, scores):
            row_max = jnp.max(scores, axis=0, keepdims=True)
            powers = jnp.exp2((scores - row_max) * EXP2_SCALE)
            prob = powers * (1.0 / jnp.sum(powers, axis=0, keepdims=True))
            rounded = prob.astype(BF16)
            out_t = lax.dot_general(value_t, rounded, NN, preferred_element_type=F32)
            att_ref[:, cols] = jnp.where(live, out_t.T, 0.0).astype(BF16)
            prob_grad = lax.dot_general(value, cotangent, NT, preferred_element_type=F32)
            delta = jnp.sum(prob * prob_grad, axis=0, keepdims=True)
            score_grad = (prob * (prob_grad - delta)).astype(BF16)
            dq_t = lax.dot_general(key_t, score_grad, NN, preferred_element_type=F32)
            dq_ref[:, cols] = (dq_t.T * SCALE).astype(BF16)
            grads.append(score_grad)
            probs.append(rounded)
            queries.append(query)
            cotangents.append(cotangent)

        held = scores_of(0)
        for head in range(heads):
            ahead = scores_of(head + 1) if head + 1 < heads else None
            finish(*held)
            held = ahead
        dk_sum[:length] += jnp.dot(
            jnp.concatenate(grads, axis=1),
            jnp.concatenate(queries, axis=0),
            preferred_element_type=F32,
        )
        dv_sum[:length] += jnp.dot(
            jnp.concatenate(probs, axis=1),
            jnp.concatenate(cotangents, axis=0),
            preferred_element_type=F32,
        )

    for count in range(1, TILES + 1):
        pl.when(ctl_ref[0] == count)(functools.partial(run, count * (img // TILES)))

    @pl.when(step == steps - 1)
    def _():
        dkv_ref[:, :HEAD_DIM] = (dk_sum[...] * SCALE).astype(BF16)
        dkv_ref[:, HEAD_DIM:] = dv_sum[...].astype(BF16)


def attend(ctl, queries, out_grad, keys_values):
    rows, width = queries.shape
    img, pairs = keys_values.shape
    groups = pairs // (2 * HEAD_DIM)
    heads = 2
    steps = width // groups // HEAD_DIM // heads
    cols = pl.BlockSpec((rows, heads * HEAD_DIM), lambda g, h, ctl: (0, g * steps + h))
    pair = pl.BlockSpec((img, 2 * HEAD_DIM), lambda g, h, ctl: (0, g))
    big = jax.ShapeDtypeStruct((rows, width), BF16)
    return pl.pallas_call(
        functools.partial(attend_kernel, heads=heads),
        grid_spec=pltpu.PrefetchScalarGridSpec(
            num_scalar_prefetch=1,
            grid=(groups, steps),
            in_specs=[cols, cols, pair],
            out_specs=[cols, cols, pair],
            scratch_shapes=[pltpu.VMEM((HEAD_DIM, img), BF16)] * 2
            + [pltpu.VMEM((img, HEAD_DIM), F32)] * 2,
        ),
        out_shape=[big, big, jax.ShapeDtypeStruct((img, pairs), BF16)],
        compiler_params=params(2),
        cost_estimate=pl.CostEstimate(
            flops=24 * rows * width * img, bytes_accessed=8 * rows * width, transcendentals=0
        ),
        name="attend",
    )(ctl, queries, out_grad, keys_values)


def norm_back_kernel(ctl_ref, parts_ref, pre_ref, gain_ref, out_ref):
    grad = jnp.sum(parts_ref[...].astype(F32), axis=0)
    tokens, width = grad.shape
    place = 1 - ctl_ref[3]
    half = LANES // 2
    lane = lax.broadcasted_iota(jnp.int32, (tokens, LANES), 1)
    blocks = pre_ref.shape[1] // 2

    def piece(block):
        high = pre_ref[:, block].astype(F32).reshape(tokens, LANES)
        low = pre_ref[:, blocks + block].astype(F32).reshape(tokens, LANES)
        held = high + low
        return jnp.where(place == block % 2, held, pltpu.roll(held, half, axis=1))

    for group in range(width // (2 * HEAD_DIM)):
        head = jnp.where(lane < half, piece(2 * group), piece(2 * group + 1))
        at = 2 * group * HEAD_DIM
        key_grad = grad[:, at : at + HEAD_DIM]
        factor = lax.rsqrt(jnp.mean(head * head, axis=-1, keepdims=True) + EPSILON)
        gained = gain_ref[...] * key_grad
        inner = jnp.mean(head * gained, axis=-1, keepdims=True)
        pre_grad = (factor * gained - factor * factor * factor * head * inner).astype(BF16)
        value_grad = grad[:, at + HEAD_DIM : at + 2 * HEAD_DIM].astype(BF16)
        for copy in range(out_ref.shape[0]):
            out_ref[copy, :, at : at + HEAD_DIM] = pre_grad
            out_ref[copy, :, at + HEAD_DIM : at + 2 * HEAD_DIM] = value_grad


def norm_back(ctl, parts, windows, gain, copies):
    tokens, width = parts.shape[1:]
    sources, rows, own, lanes = windows.shape
    last = lanes // LANES - 1
    return pl.pallas_call(
        norm_back_kernel,
        grid_spec=pltpu.PrefetchScalarGridSpec(
            num_scalar_prefetch=1,
            grid=(1,),
            in_specs=[
                whole(parts.shape),
                pl.BlockSpec(
                    (sources, rows, own, LANES), lambda i, ctl: (0, 0, 0, last * (1 - ctl[3]))
                ),
                whole(gain.shape),
            ],
            out_specs=whole((copies, tokens, width)),
        ),
        out_shape=jax.ShapeDtypeStruct((copies, tokens, width), BF16),
        name="norm_back",
    )(ctl, parts, windows, gain)


def turn_kernel(ctl_ref, f_ref, out_ref):
    odd = ctl_ref[3]
    turned = f_ref[...].reshape(-1, f_ref.shape[-1]).T
    rows = out_ref.shape[0]
    spare = turned.shape[0] - rows

    @pl.when(odd == 0)
    def _():
        out_ref[...] = turned[:rows]

    @pl.when(odd != 0)
    def _():
        out_ref[...] = turned[spare:]


def turn(ctl, windows, feat):
    sources, rows, own, width = windows.shape
    tokens = sources * own
    return pl.pallas_call(
        turn_kernel,
        grid_spec=pltpu.PrefetchScalarGridSpec(
            num_scalar_prefetch=1,
            grid=(rows,),
            in_specs=[pl.BlockSpec((sources, 1, own, width), lambda r, ctl: (0, r, 0, 0))],
            out_specs=pl.BlockSpec((feat, tokens), lambda r, ctl: (0, r)),
        ),
        out_shape=jax.ShapeDtypeStruct((feat, rows * tokens), BF16),
        compiler_params=params(1),
        name="turn",
    )(ctl, windows)


def weight_kernel(f_ref, g_ref, out_ref):
    out_ref[...] = jnp.dot(f_ref[...], g_ref[...], preferred_element_type=F32).astype(BF16)


def weight_grad(turned, grads):
    feat, tokens = turned.shape
    width = grads.shape[1]
    return pl.pallas_call(
        weight_kernel,
        out_shape=jax.ShapeDtypeStruct((feat, width), BF16),
        compiler_params=pltpu.CompilerParams(vmem_limit_bytes=VMEM_LIMIT),
        cost_estimate=pl.CostEstimate(
            flops=2 * feat * tokens * width, bytes_accessed=2 * feat * tokens, transcendentals=0
        ),
        name="weight_grad",
    )(turned, grads)


def finish_kernel(parts_ref, key_ref, value_ref):
    total = jnp.sum(parts_ref[...].astype(F32), axis=0)
    for group in range(total.shape[1] // (2 * HEAD_DIM)):
        cols = slice(group * HEAD_DIM, (group + 1) * HEAD_DIM)
        at = 2 * group * HEAD_DIM
        key_ref[:, cols] = total[:, at : at + HEAD_DIM]
        value_ref[:, cols] = total[:, at + HEAD_DIM : at + 2 * HEAD_DIM]


def finish(parts):
    out = jax.ShapeDtypeStruct((parts.shape[1], parts.shape[2] // 2), F32)
    return pl.pallas_call(finish_kernel, out_shape=[out, out], name="finish")(parts)


def exchange(array, axes):
    return lax.all_to_all(array, axes, split_axis=0, concat_axis=0, tiled=True)


def on_device(queries, features, w_key, w_value, key_gain, out_grad, tile_counts, text_start):
    dp, seq = lax.axis_size("dp"), lax.axis_size("seq")
    rows, own, feat = features.shape
    text_dev = queries.shape[1]
    pairs = 2 * w_key.shape[1]
    tokens = rows * own
    gain = key_gain.reshape(1, HEAD_DIM)
    dp_index, seq_index = lax.axis_index("dp"), lax.axis_index("seq")
    ctl = jnp.stack([tile_counts[0], seq_index * text_dev, text_start[0], dp_index & 1])
    feats = features.reshape(tokens, feat)
    send, windows = project(feats, w_key, w_value, gain, dp, seq)
    arrived = exchange(send.reshape(seq * dp, own, pairs), ("seq", "dp"))
    windows, arrived = lax.optimization_barrier((windows, arrived))
    keys_values = arrived.reshape(seq * tokens, pairs)
    windows = exchange(windows, "dp").reshape(dp, rows, own, -1)
    attended, query_grad, grads = attend(ctl, queries[0], out_grad[0], keys_values)
    shares = exchange(grads.reshape(seq, tokens, pairs), "seq")
    turned = turn(ctl, windows, feat // dp)
    rounded = norm_back(ctl, shares, windows, gain, dp)
    everywhere = exchange(rounded, "dp").reshape(dp * tokens, pairs)
    partial = weight_grad(turned, everywhere)
    pieces = exchange(partial.reshape(seq, feat // dp // seq, pairs), "seq")
    key_weight, value_weight = finish(pieces)
    return attended[None], query_grad[None], key_weight, value_weight


def solution(mesh):
    placed = (
        P("dp", "seq", "mp"),
        P(None, ("seq", "dp"), None),
        P(None, "mp"),
        P(None, "mp"),
        P(),
        P("dp", "seq", "mp"),
        P("dp"),
        P("dp"),
    )
    return jax.shard_map(
        on_device,
        mesh=mesh,
        in_specs=placed,
        out_specs=(
            P("dp", "seq", "mp"),
            P("dp", "seq", "mp"),
            P(("dp", "seq"), "mp"),
            P(("dp", "seq"), "mp"),
        ),
        check_vma=False,
    )
```

```python
import functools

import jax
import jax.numpy as jnp
from jax import lax
from jax.experimental import pallas as pl
from jax.experimental.pallas import tpu as pltpu
from jax.sharding import PartitionSpec as P

HEAD_DIM = 128
TILES = 4
EPSILON = 1e-05
SCALE = HEAD_DIM**-0.5
EXP2_SCALE = SCALE * 1.4426950408889634
BF16 = jnp.bfloat16
F32 = jnp.float32
LANES = 128
SUBLANES = 8
CHUNK = 128
VMEM_LIMIT = 59 * 2**20
SMALL_LIMIT = 16 * 2**20

NN = (((1,), (0,)), ((), ()))
NT = (((1,), (1,)), ((), ()))


def whole(shape):
    return pl.BlockSpec(shape, lambda *_: (0,) * len(shape))


def params(axes, limit=VMEM_LIMIT):
    return pltpu.CompilerParams(
        vmem_limit_bytes=limit, dimension_semantics=("arbitrary",) * axes
    )


def project_kernel(f_ref, wk_ref, wv_ref, gain_ref, send_ref, pre_ref, total):
    step, steps = pl.program_id(0), pl.num_programs(0)
    kv_dim = wk_ref.shape[1]

    @pl.when(step == 0)
    def _():
        total[...] = jnp.zeros_like(total)

    total[:, :kv_dim] += jnp.dot(f_ref[...], wk_ref[...], preferred_element_type=F32)
    total[:, kv_dim:] += jnp.dot(f_ref[...], wv_ref[...], preferred_element_type=F32)

    @pl.when(step == steps - 1)
    def _():
        pre_ref[...] = total[:, :kv_dim]
        for group in range(kv_dim // HEAD_DIM):
            cols = slice(group * HEAD_DIM, (group + 1) * HEAD_DIM)
            head = total[:, cols]
            factor = lax.rsqrt(jnp.mean(head * head, axis=-1, keepdims=True) + EPSILON)
            key = (head * factor * gain_ref[...]).astype(BF16)
            start = kv_dim + group * HEAD_DIM
            value = total[:, start : start + HEAD_DIM].astype(BF16)
            at = 2 * group * HEAD_DIM
            for copy in range(send_ref.shape[0]):
                send_ref[copy, :, at : at + HEAD_DIM] = key
                send_ref[copy, :, at + HEAD_DIM : at + 2 * HEAD_DIM] = value


def project(feats, w_key, w_value, gain, copies):
    tokens, feat = feats.shape
    kv_dim = w_key.shape[1]
    steps = 5
    depth = feat // steps
    send, pre = (copies, tokens, 2 * kv_dim), (tokens, kv_dim)
    return pl.pallas_call(
        project_kernel,
        grid=(steps,),
        in_specs=[
            pl.BlockSpec((tokens, depth), lambda k: (0, k)),
            pl.BlockSpec((depth, kv_dim), lambda k: (k, 0)),
            pl.BlockSpec((depth, kv_dim), lambda k: (k, 0)),
            whole((1, HEAD_DIM)),
        ],
        out_specs=[whole(send), whole(pre)],
        out_shape=[jax.ShapeDtypeStruct(send, BF16), jax.ShapeDtypeStruct(pre, F32)],
        scratch_shapes=[pltpu.VMEM((tokens, 2 * kv_dim), F32)],
        compiler_params=params(1),
        cost_estimate=pl.CostEstimate(
            flops=4 * tokens * feat * kv_dim,
            bytes_accessed=4 * feat * kv_dim + 4 * tokens * feat,
            transcendentals=0,
        ),
        name="project",
    )(feats, w_key, w_value, gain)


def cut_kernel(f_ref, pre_ref, win_ref):
    windows, tokens, width = win_ref.shape
    tiles = f_ref.shape[1] // LANES
    own = tokens // windows
    half = LANES // 2
    lane = lax.broadcasted_iota(jnp.int32, (own, LANES), 1)
    for window in range(windows):
        tile = window * tiles // windows
        win_ref[window] = f_ref[:, tile * LANES : tile * LANES + width]
        head = pre_ref[window * own : (window + 1) * own]
        high = head.astype(BF16).astype(F32)
        pair = jnp.concatenate([high, head - high], axis=1)
        place = 1 - window % 2
        at = (width - LANES) * place
        for block in range(windows):
            piece = pair[:, block // 2 * LANES : (block // 2 + 1) * LANES]
            if block % 2 != place:
                piece = pltpu.roll(piece, half, axis=1)
            rows = slice(block * own, (block + 1) * own)
            kept = win_ref[window, rows, at : at + LANES].astype(F32)
            mixed = jnp.where((lane >= half) == bool(place), piece, kept)
            win_ref[window, rows, at : at + LANES] = mixed.astype(BF16)


def cut(feats, key_pre, windows):
    tokens, feat = feats.shape
    width = -(-(feat // windows) // LANES) * LANES
    return pl.pallas_call(
        cut_kernel,
        out_shape=jax.ShapeDtypeStruct((windows, tokens, width), BF16),
        compiler_params=params(0, SMALL_LIMIT),
        cost_estimate=pl.CostEstimate(
            flops=0, bytes_accessed=6 * tokens * feat, transcendentals=0
        ),
        name="cut",
    )(feats, key_pre)


def attend_kernel(
    ctl_ref, q_ref, d_ref, kv_ref, prob_ref, grad_ref, dkv_ref, dk_sum, dv_sum, powers_ref, live_ref, *, heads
):
    step, steps = pl.program_id(1), pl.num_programs(1)
    rows = q_ref.shape[0]
    img = kv_ref.shape[0]

    @pl.when(step == 0)
    def _():
        dk_sum[...] = jnp.zeros_like(dk_sum)
        dv_sum[...] = jnp.zeros_like(dv_sum)

    def run(length):
        position = ctl_ref[1] + lax.broadcasted_iota(jnp.int32, (rows, HEAD_DIM), 0)
        live = position >= ctl_ref[2]
        chunks = [slice(at, at + CHUNK) for at in range(0, length, CHUNK)]
        folded = (CHUNK // SUBLANES, SUBLANES, rows)

        def against(chunk, start, other):
            left = kv_ref[chunk, start : start + HEAD_DIM]
            out = lax.dot_general(left, other, NT, preferred_element_type=F32)
            return out.reshape(folded)

        def first(head):
            cols = slice(head * HEAD_DIM, (head + 1) * HEAD_DIM)
            here = slice(head * rows, (head + 1) * rows)
            query = q_ref[:, cols]
            cotangent = jnp.where(live, d_ref[:, cols], jnp.zeros((), BF16))
            live_ref[here] = cotangent
            tops, sums, deltas = [], [], []
            for chunk in chunks:
                scores = against(chunk, 0, query)
                top = jnp.max(scores, axis=0)
                powers = jnp.exp2((scores - top[None]) * EXP2_SCALE)
                powers_ref[chunk, here] = powers.reshape(CHUNK, rows)
                tops.append(top)
                sums.append(jnp.sum(powers, axis=0))
                deltas.append(jnp.sum(powers * against(chunk, HEAD_DIM, cotangent), axis=0))
            row_max = jnp.max(functools.reduce(jnp.maximum, tops), axis=0, keepdims=True)
            factors = [jnp.exp2((top - row_max) * EXP2_SCALE) for top in tops]

            def over_rows(parts):
                total = sum(part * factor for part, factor in zip(parts, factors))
                return jnp.sum(total, axis=0, keepdims=True)

            inverse = 1.0 / over_rows(sums)
            delta = over_rows(deltas) * inverse
            return cotangent, here, [factor * inverse for factor in factors], delta

        def second(cotangent, here, factors, delta):
            for chunk, factor in zip(chunks, factors):
                prob = powers_ref[chunk, here].reshape(folded) * factor[None]
                prob_ref[chunk, here] = prob.reshape(CHUNK, rows).astype(BF16)
                score_grad = prob * (against(chunk, HEAD_DIM, cotangent) - delta[None])
                grad_ref[chunk, here] = score_grad.reshape(CHUNK, rows).astype(BF16)

        held = first(0)
        for head in range(heads):
            ahead = first(head + 1) if head + 1 < heads else None
            second(*held)
            held = ahead
        queries = jnp.concatenate(
            [q_ref[:, head * HEAD_DIM : (head + 1) * HEAD_DIM] for head in range(heads)], axis=0
        )
        dk_sum[:length] += jnp.dot(grad_ref[:length], queries, preferred_element_type=F32)
        dv_sum[:length] += jnp.dot(prob_ref[:length], live_ref[...], preferred_element_type=F32)

    for count in range(1, TILES + 1):
        pl.when(ctl_ref[0] == count)(functools.partial(run, count * (img // TILES)))

    @pl.when(step == steps - 1)
    def _():
        dkv_ref[:, :HEAD_DIM] = (dk_sum[...] * SCALE).astype(BF16)
        dkv_ref[:, HEAD_DIM:] = dv_sum[...].astype(BF16)


def attend(ctl, queries, out_grad, keys_values):
    rows, width = queries.shape
    img, pairs = keys_values.shape
    groups = pairs // (2 * HEAD_DIM)
    heads = 2
    steps = width // groups // HEAD_DIM // heads
    cols = pl.BlockSpec((rows, heads * HEAD_DIM), lambda g, h, ctl: (0, g * steps + h))
    pair = pl.BlockSpec((img, 2 * HEAD_DIM), lambda g, h, ctl: (0, g))
    square = pl.BlockSpec((img, heads * rows), lambda g, h, ctl: (0, g * steps + h))
    big = jax.ShapeDtypeStruct((img, width // HEAD_DIM * rows), BF16)
    return pl.pallas_call(
        functools.partial(attend_kernel, heads=heads),
        grid_spec=pltpu.PrefetchScalarGridSpec(
            num_scalar_prefetch=1,
            grid=(groups, steps),
            in_specs=[cols, cols, pair],
            out_specs=[square, square, pair],
            scratch_shapes=[pltpu.VMEM((img, HEAD_DIM), F32)] * 2
            + [
                pltpu.VMEM((img, heads * rows), F32),
                pltpu.VMEM((heads * rows, HEAD_DIM), BF16),
            ],
        ),
        out_shape=[big, big, jax.ShapeDtypeStruct((img, pairs), BF16)],
        compiler_params=params(2),
        cost_estimate=pl.CostEstimate(
            flops=20 * rows * width * img, bytes_accessed=8 * rows * width, transcendentals=0
        ),
        name="attend",
    )(ctl, queries, out_grad, keys_values)


def apply_kernel(ctl_ref, left_ref, kv_ref, out_ref, turned_ref, *, heads, start, masked):
    rows = out_ref.shape[0]
    img = kv_ref.shape[0]

    @pl.when(pl.program_id(1) == 0)
    def _():
        turned_ref[...] = kv_ref[:, start : start + HEAD_DIM].T

    def run(length):
        position = ctl_ref[1] + lax.broadcasted_iota(jnp.int32, (rows, HEAD_DIM), 0)
        live = position >= ctl_ref[2]
        for head in range(heads):
            left = left_ref[:length, head * rows : (head + 1) * rows]
            out = jnp.dot(turned_ref[:, :length], left, preferred_element_type=F32).T
            out = jnp.where(live, out, 0.0) if masked else out * SCALE
            out_ref[:, head * HEAD_DIM : (head + 1) * HEAD_DIM] = out.astype(BF16)

    for count in range(1, TILES + 1):
        pl.when(ctl_ref[0] == count)(functools.partial(run, count * (img // TILES)))


def apply(ctl, left, keys_values, rows, start, masked, name):
    img, pairs = keys_values.shape
    groups = pairs // (2 * HEAD_DIM)
    heads = 2
    all_heads = left.shape[1] // rows
    steps = all_heads // groups // heads
    return pl.pallas_call(
        functools.partial(apply_kernel, heads=heads, start=start, masked=masked),
        grid_spec=pltpu.PrefetchScalarGridSpec(
            num_scalar_prefetch=1,
            grid=(groups, steps),
            in_specs=[
                pl.BlockSpec((img, heads * rows), lambda g, h, ctl: (0, g * steps + h)),
                pl.BlockSpec((img, 2 * HEAD_DIM), lambda g, h, ctl: (0, g)),
            ],
            out_specs=pl.BlockSpec((rows, heads * HEAD_DIM), lambda g, h, ctl: (0, g * steps + h)),
            scratch_shapes=[pltpu.VMEM((HEAD_DIM, img), BF16)],
        ),
        out_shape=jax.ShapeDtypeStruct((rows, all_heads * HEAD_DIM), BF16),
        compiler_params=params(2),
        cost_estimate=pl.CostEstimate(
            flops=2 * img * rows * all_heads * HEAD_DIM,
            bytes_accessed=2 * img * rows * all_heads,
            transcendentals=0,
        ),
        name=name,
    )(ctl, left, keys_values)


def norm_back_kernel(ctl_ref, parts_ref, pre_ref, gain_ref, out_ref):
    grad = jnp.sum(parts_ref[...].astype(F32), axis=0)
    tokens, width = grad.shape
    place = 1 - ctl_ref[3]
    half = LANES // 2
    lane = lax.broadcasted_iota(jnp.int32, (tokens, LANES), 1)
    blocks = pre_ref.shape[1] // 2

    def piece(block):
        high = pre_ref[:, block].astype(F32).reshape(tokens, LANES)
        low = pre_ref[:, blocks + block].astype(F32).reshape(tokens, LANES)
        held = high + low
        return jnp.where(place == block % 2, held, pltpu.roll(held, half, axis=1))

    for group in range(width // (2 * HEAD_DIM)):
        head = jnp.where(lane < half, piece(2 * group), piece(2 * group + 1))
        at = 2 * group * HEAD_DIM
        key_grad = grad[:, at : at + HEAD_DIM]
        factor = lax.rsqrt(jnp.mean(head * head, axis=-1, keepdims=True) + EPSILON)
        gained = gain_ref[...] * key_grad
        inner = jnp.mean(head * gained, axis=-1, keepdims=True)
        pre_grad = (factor * gained - factor * factor * factor * head * inner).astype(BF16)
        value_grad = grad[:, at + HEAD_DIM : at + 2 * HEAD_DIM].astype(BF16)
        for copy in range(out_ref.shape[0]):
            out_ref[copy, :, at : at + HEAD_DIM] = pre_grad
            out_ref[copy, :, at + HEAD_DIM : at + 2 * HEAD_DIM] = value_grad


def norm_back(ctl, parts, windows, gain, copies):
    tokens, width = parts.shape[1:]
    sources, rows, own, lanes = windows.shape
    last = lanes // LANES - 1
    return pl.pallas_call(
        norm_back_kernel,
        grid_spec=pltpu.PrefetchScalarGridSpec(
            num_scalar_prefetch=1,
            grid=(1,),
            in_specs=[
                whole(parts.shape),
                pl.BlockSpec(
                    (sources, rows, own, LANES), lambda i, ctl: (0, 0, 0, last * (1 - ctl[3]))
                ),
                whole(gain.shape),
            ],
            out_specs=whole((copies, tokens, width)),
        ),
        out_shape=jax.ShapeDtypeStruct((copies, tokens, width), BF16),
        compiler_params=params(1, SMALL_LIMIT),
        name="norm_back",
    )(ctl, parts, windows, gain)


def turn_kernel(ctl_ref, f_ref, out_ref):
    odd = ctl_ref[3]
    turned = f_ref[...].reshape(-1, f_ref.shape[-1]).T
    rows = out_ref.shape[0]
    spare = turned.shape[0] - rows

    @pl.when(odd == 0)
    def _():
        out_ref[...] = turned[:rows]

    @pl.when(odd != 0)
    def _():
        out_ref[...] = turned[spare:]


def turn(ctl, windows, feat):
    sources, rows, own, width = windows.shape
    tokens = sources * own
    return pl.pallas_call(
        turn_kernel,
        grid_spec=pltpu.PrefetchScalarGridSpec(
            num_scalar_prefetch=1,
            grid=(rows,),
            in_specs=[pl.BlockSpec((sources, 1, own, width), lambda r, ctl: (0, r, 0, 0))],
            out_specs=pl.BlockSpec((feat, tokens), lambda r, ctl: (0, r)),
        ),
        out_shape=jax.ShapeDtypeStruct((feat, rows * tokens), BF16),
        compiler_params=params(1, SMALL_LIMIT),
        name="turn",
    )(ctl, windows)


def weight_kernel(f_ref, g_ref, out_ref):
    out_ref[...] = jnp.dot(f_ref[...], g_ref[...], preferred_element_type=F32).astype(BF16)


def weight_grad(turned, grads):
    feat, tokens = turned.shape
    width = grads.shape[1]
    return pl.pallas_call(
        weight_kernel,
        out_shape=jax.ShapeDtypeStruct((feat, width), BF16),
        compiler_params=params(0, SMALL_LIMIT),
        cost_estimate=pl.CostEstimate(
            flops=2 * feat * tokens * width, bytes_accessed=2 * feat * tokens, transcendentals=0
        ),
        name="weight_grad",
    )(turned, grads)


def finish_kernel(parts_ref, key_ref, value_ref):
    total = jnp.sum(parts_ref[...].astype(F32), axis=0)
    for group in range(total.shape[1] // (2 * HEAD_DIM)):
        cols = slice(group * HEAD_DIM, (group + 1) * HEAD_DIM)
        at = 2 * group * HEAD_DIM
        key_ref[:, cols] = total[:, at : at + HEAD_DIM]
        value_ref[:, cols] = total[:, at + HEAD_DIM : at + 2 * HEAD_DIM]


def finish(parts):
    out = jax.ShapeDtypeStruct((parts.shape[1], parts.shape[2] // 2), F32)
    return pl.pallas_call(
        finish_kernel,
        out_shape=[out, out],
        compiler_params=params(0, SMALL_LIMIT),
        name="finish",
    )(parts)


def exchange(array, axes):
    return lax.all_to_all(array, axes, split_axis=0, concat_axis=0, tiled=True)


def on_device(queries, features, w_key, w_value, key_gain, out_grad, tile_counts, text_start):
    dp, seq = lax.axis_size("dp"), lax.axis_size("seq")
    rows, own, feat = features.shape
    text_dev = queries.shape[1]
    pairs = 2 * w_key.shape[1]
    tokens = rows * own
    gain = key_gain.reshape(1, HEAD_DIM)
    dp_index, seq_index = lax.axis_index("dp"), lax.axis_index("seq")
    ctl = jnp.stack([tile_counts[0], seq_index * text_dev, text_start[0], dp_index & 1])
    feats = features.reshape(tokens, feat)
    send, key_pre = project(feats, w_key, w_value, gain, seq)
    windows = cut(feats, key_pre, dp)
    arrived = exchange(send.reshape(seq * dp, own, pairs), ("seq", "dp"))
    windows, arrived, ctl = lax.optimization_barrier((windows, arrived, ctl))
    keys_values = arrived.reshape(seq * tokens, pairs)
    windows = exchange(windows, "dp").reshape(dp, rows, own, -1)
    probs, score_grads, grads = attend(ctl, queries[0], out_grad[0], keys_values)
    grads, windows = lax.optimization_barrier((grads, windows))
    shares = exchange(grads.reshape(seq, tokens, pairs), "seq")
    attended = apply(ctl, probs, keys_values, text_dev, HEAD_DIM, True, "attended")
    shares, attended = lax.optimization_barrier((shares, attended))
    rounded = norm_back(ctl, shares, windows, gain, dp)
    everywhere = exchange(rounded, "dp").reshape(dp * tokens, pairs)
    turned = turn(ctl, windows, feat // dp)
    query_grad = apply(ctl, score_grads, keys_values, text_dev, 0, False, "query_grad")
    everywhere, query_grad = lax.optimization_barrier((everywhere, query_grad))
    partial = weight_grad(turned, everywhere)
    pieces = exchange(partial.reshape(seq, feat // dp // seq, pairs), "seq")
    key_weight, value_weight = finish(pieces)
    return attended[None], query_grad[None], key_weight, value_weight


def solution(mesh):
    placed = (
        P("dp", "seq", "mp"),
        P(None, ("seq", "dp"), None),
        P(None, "mp"),
        P(None, "mp"),
        P(),
        P("dp", "seq", "mp"),
        P("dp"),
        P("dp"),
    )
    return jax.shard_map(
        on_device,
        mesh=mesh,
        in_specs=placed,
        out_specs=(
            P("dp", "seq", "mp"),
            P("dp", "seq", "mp"),
            P(("dp", "seq"), "mp"),
            P(("dp", "seq"), "mp"),
        ),
        check_vma=False,
    )
```

```python
import functools

import jax
import jax.numpy as jnp
from jax import lax
from jax.experimental import pallas as pl
from jax.experimental.pallas import tpu as pltpu
from jax.sharding import PartitionSpec as P

HEAD_DIM = 128
TILES = 4
EPSILON = 1e-05
SCALE = HEAD_DIM**-0.5
EXP2_SCALE = SCALE * 1.4426950408889634
BF16 = jnp.bfloat16
F32 = jnp.float32
LANES = 128
SUBLANES = 8
CHUNK = 128
VMEM_LIMIT = 59 * 2**20
SMALL_LIMIT = 16 * 2**20

NN = (((1,), (0,)), ((), ()))
NT = (((1,), (1,)), ((), ()))


def whole(shape):
    return pl.BlockSpec(shape, lambda *_: (0,) * len(shape))


def params(axes, limit=VMEM_LIMIT):
    return pltpu.CompilerParams(
        vmem_limit_bytes=limit, dimension_semantics=("arbitrary",) * axes
    )


def project_kernel(
    f_hbm, wk_hbm, wv_hbm, gain_ref, send_ref, pre_ref, f_ref, wk_ref, wv_ref, arrived, *, parts
):
    tokens, feat = f_ref.shape
    kv_dim = wk_ref.shape[1]
    depth = feat // parts
    copies = []
    for part in range(parts):
        here = pl.ds(part * depth, depth)
        copies.append(
            [
                pltpu.make_async_copy(f_hbm.at[:, here], f_ref.at[:, here], arrived.at[0, part]),
                pltpu.make_async_copy(wk_hbm.at[here], wk_ref.at[here], arrived.at[1, part]),
                pltpu.make_async_copy(wv_hbm.at[here], wv_ref.at[here], arrived.at[2, part]),
            ]
        )
    for trio in copies:
        for copy in trio:
            copy.start()
    keys = jnp.zeros((tokens, kv_dim), F32)
    values = jnp.zeros((tokens, kv_dim), F32)
    for part, trio in enumerate(copies):
        here = slice(part * depth, (part + 1) * depth)
        for copy in trio:
            copy.wait()
        left = f_ref[:, here]
        keys += jnp.dot(left, wk_ref[here], preferred_element_type=F32)
        values += jnp.dot(left, wv_ref[here], preferred_element_type=F32)
    pre_ref[...] = keys
    for group in range(kv_dim // HEAD_DIM):
        cols = slice(group * HEAD_DIM, (group + 1) * HEAD_DIM)
        head = keys[:, cols]
        factor = lax.rsqrt(jnp.mean(head * head, axis=-1, keepdims=True) + EPSILON)
        key = (head * factor * gain_ref[...]).astype(BF16)
        value = values[:, cols].astype(BF16)
        at = 2 * group * HEAD_DIM
        for copy in range(send_ref.shape[0]):
            send_ref[copy, :, at : at + HEAD_DIM] = key
            send_ref[copy, :, at + HEAD_DIM : at + 2 * HEAD_DIM] = value


def project(feats, w_key, w_value, gain, copies):
    tokens, feat = feats.shape
    kv_dim = w_key.shape[1]
    parts = 6
    send, pre = (copies, tokens, 2 * kv_dim), (tokens, kv_dim)
    anywhere = pl.BlockSpec(memory_space=pl.ANY)
    return pl.pallas_call(
        functools.partial(project_kernel, parts=parts),
        in_specs=[anywhere, anywhere, anywhere, pl.BlockSpec(memory_space=pltpu.VMEM)],
        out_shape=[jax.ShapeDtypeStruct(send, BF16), jax.ShapeDtypeStruct(pre, F32)],
        scratch_shapes=[
            pltpu.VMEM((tokens, feat), BF16),
            pltpu.VMEM((feat, kv_dim), BF16),
            pltpu.VMEM((feat, kv_dim), BF16),
            pltpu.SemaphoreType.DMA((3, parts)),
        ],
        compiler_params=params(0),
        cost_estimate=pl.CostEstimate(
            flops=4 * tokens * feat * kv_dim,
            bytes_accessed=4 * feat * kv_dim + 4 * tokens * feat,
            transcendentals=0,
        ),
        name="project",
    )(feats, w_key, w_value, gain)


def cut_kernel(f_ref, pre_ref, win_ref):
    windows, tokens, width = win_ref.shape
    tiles = f_ref.shape[1] // LANES
    own = tokens // windows
    half = LANES // 2
    lane = lax.broadcasted_iota(jnp.int32, (own, LANES), 1)
    for window in range(windows):
        tile = window * tiles // windows
        win_ref[window] = f_ref[:, tile * LANES : tile * LANES + width]
        head = pre_ref[window * own : (window + 1) * own]
        high = head.astype(BF16).astype(F32)
        pair = jnp.concatenate([high, head - high], axis=1)
        place = 1 - window % 2
        at = (width - LANES) * place
        for block in range(windows):
            piece = pair[:, block // 2 * LANES : (block // 2 + 1) * LANES]
            if block % 2 != place:
                piece = pltpu.roll(piece, half, axis=1)
            rows = slice(block * own, (block + 1) * own)
            kept = win_ref[window, rows, at : at + LANES].astype(F32)
            mixed = jnp.where((lane >= half) == bool(place), piece, kept)
            win_ref[window, rows, at : at + LANES] = mixed.astype(BF16)


def cut(feats, key_pre, windows):
    tokens, feat = feats.shape
    width = -(-(feat // windows) // LANES) * LANES
    return pl.pallas_call(
        cut_kernel,
        out_shape=jax.ShapeDtypeStruct((windows, tokens, width), BF16),
        compiler_params=params(0, SMALL_LIMIT),
        cost_estimate=pl.CostEstimate(
            flops=0, bytes_accessed=6 * tokens * feat, transcendentals=0
        ),
        name="cut",
    )(feats, key_pre)


def attend_kernel(
    ctl_ref, q_ref, d_ref, kv_ref, prob_ref, grad_ref, dkv_ref, dk_sum, dv_sum, powers_ref, live_ref, *, heads
):
    step, steps = pl.program_id(1), pl.num_programs(1)
    rows = q_ref.shape[0]
    img = kv_ref.shape[0]

    @pl.when(step == 0)
    def _():
        dk_sum[...] = jnp.zeros_like(dk_sum)
        dv_sum[...] = jnp.zeros_like(dv_sum)

    def run(length):
        position = ctl_ref[1] + lax.broadcasted_iota(jnp.int32, (rows, HEAD_DIM), 0)
        live = position >= ctl_ref[2]
        chunks = [slice(at, at + CHUNK) for at in range(0, length, CHUNK)]
        folded = (CHUNK // SUBLANES, SUBLANES, rows)

        def against(chunk, start, other):
            left = kv_ref[chunk, start : start + HEAD_DIM]
            out = lax.dot_general(left, other, NT, preferred_element_type=F32)
            return out.reshape(folded)

        def first(head):
            cols = slice(head * HEAD_DIM, (head + 1) * HEAD_DIM)
            here = slice(head * rows, (head + 1) * rows)
            query = q_ref[:, cols]
            cotangent = jnp.where(live, d_ref[:, cols], jnp.zeros((), BF16))
            live_ref[here] = cotangent
            tops, sums, deltas = [], [], []
            for chunk in chunks:
                scores = against(chunk, 0, query)
                top = jnp.max(scores, axis=0)
                powers = jnp.exp2((scores - top[None]) * EXP2_SCALE)
                powers_ref[chunk, here] = powers.reshape(CHUNK, rows)
                tops.append(top)
                sums.append(jnp.sum(powers, axis=0))
                deltas.append(jnp.sum(powers * against(chunk, HEAD_DIM, cotangent), axis=0))
            row_max = jnp.max(functools.reduce(jnp.maximum, tops), axis=0, keepdims=True)
            factors = [jnp.exp2((top - row_max) * EXP2_SCALE) for top in tops]

            def over_rows(parts):
                total = sum(part * factor for part, factor in zip(parts, factors))
                return jnp.sum(total, axis=0, keepdims=True)

            inverse = 1.0 / over_rows(sums)
            delta = over_rows(deltas) * inverse
            return cotangent, here, [factor * inverse for factor in factors], delta

        def second(cotangent, here, factors, delta):
            for chunk, factor in zip(chunks, factors):
                prob = powers_ref[chunk, here].reshape(folded) * factor[None]
                prob_ref[chunk, here] = prob.reshape(CHUNK, rows).astype(BF16)
                score_grad = prob * (against(chunk, HEAD_DIM, cotangent) - delta[None])
                grad_ref[chunk, here] = score_grad.reshape(CHUNK, rows).astype(BF16)

        held = first(0)
        for head in range(heads):
            ahead = first(head + 1) if head + 1 < heads else None
            second(*held)
            held = ahead
        queries = jnp.concatenate(
            [q_ref[:, head * HEAD_DIM : (head + 1) * HEAD_DIM] for head in range(heads)], axis=0
        )
        dk_sum[:length] += jnp.dot(grad_ref[:length], queries, preferred_element_type=F32)
        dv_sum[:length] += jnp.dot(prob_ref[:length], live_ref[...], preferred_element_type=F32)

    for count in range(1, TILES + 1):
        pl.when(ctl_ref[0] == count)(functools.partial(run, count * (img // TILES)))

    @pl.when(step == steps - 1)
    def _():
        dkv_ref[:, :HEAD_DIM] = (dk_sum[...] * SCALE).astype(BF16)
        dkv_ref[:, HEAD_DIM:] = dv_sum[...].astype(BF16)


def attend(ctl, queries, out_grad, keys_values):
    rows, width = queries.shape
    img, pairs = keys_values.shape
    groups = pairs // (2 * HEAD_DIM)
    heads = 2
    steps = width // groups // HEAD_DIM // heads
    cols = pl.BlockSpec((rows, heads * HEAD_DIM), lambda g, h, ctl: (0, g * steps + h))
    pair = pl.BlockSpec((img, 2 * HEAD_DIM), lambda g, h, ctl: (0, g))
    square = pl.BlockSpec((img, heads * rows), lambda g, h, ctl: (0, g * steps + h))
    big = jax.ShapeDtypeStruct((img, width // HEAD_DIM * rows), BF16)
    return pl.pallas_call(
        functools.partial(attend_kernel, heads=heads),
        grid_spec=pltpu.PrefetchScalarGridSpec(
            num_scalar_prefetch=1,
            grid=(groups, steps),
            in_specs=[cols, cols, pair],
            out_specs=[square, square, pair],
            scratch_shapes=[pltpu.VMEM((img, HEAD_DIM), F32)] * 2
            + [
                pltpu.VMEM((img, heads * rows), F32),
                pltpu.VMEM((heads * rows, HEAD_DIM), BF16),
            ],
        ),
        out_shape=[big, big, jax.ShapeDtypeStruct((img, pairs), BF16)],
        compiler_params=params(2),
        cost_estimate=pl.CostEstimate(
            flops=20 * rows * width * img, bytes_accessed=8 * rows * width, transcendentals=0
        ),
        name="attend",
    )(ctl, queries, out_grad, keys_values)


def apply_kernel(ctl_ref, left_ref, kv_ref, out_ref, turned_ref, *, heads, start, masked):
    rows = out_ref.shape[0]
    img = kv_ref.shape[0]

    @pl.when(pl.program_id(1) == 0)
    def _():
        turned_ref[...] = kv_ref[:, start : start + HEAD_DIM].T

    def run(length):
        position = ctl_ref[1] + lax.broadcasted_iota(jnp.int32, (rows, HEAD_DIM), 0)
        live = position >= ctl_ref[2]
        for head in range(heads):
            left = left_ref[:length, head * rows : (head + 1) * rows]
            out = jnp.dot(turned_ref[:, :length], left, preferred_element_type=F32).T
            out = jnp.where(live, out, 0.0) if masked else out * SCALE
            out_ref[:, head * HEAD_DIM : (head + 1) * HEAD_DIM] = out.astype(BF16)

    for count in range(1, TILES + 1):
        pl.when(ctl_ref[0] == count)(functools.partial(run, count * (img // TILES)))


def apply(ctl, left, keys_values, rows, start, masked, name):
    img, pairs = keys_values.shape
    groups = pairs // (2 * HEAD_DIM)
    heads = 2
    all_heads = left.shape[1] // rows
    steps = all_heads // groups // heads
    return pl.pallas_call(
        functools.partial(apply_kernel, heads=heads, start=start, masked=masked),
        grid_spec=pltpu.PrefetchScalarGridSpec(
            num_scalar_prefetch=1,
            grid=(groups, steps),
            in_specs=[
                pl.BlockSpec((img, heads * rows), lambda g, h, ctl: (0, g * steps + h)),
                pl.BlockSpec((img, 2 * HEAD_DIM), lambda g, h, ctl: (0, g)),
            ],
            out_specs=pl.BlockSpec((rows, heads * HEAD_DIM), lambda g, h, ctl: (0, g * steps + h)),
            scratch_shapes=[pltpu.VMEM((HEAD_DIM, img), BF16)],
        ),
        out_shape=jax.ShapeDtypeStruct((rows, all_heads * HEAD_DIM), BF16),
        compiler_params=params(2),
        cost_estimate=pl.CostEstimate(
            flops=2 * img * rows * all_heads * HEAD_DIM,
            bytes_accessed=2 * img * rows * all_heads,
            transcendentals=0,
        ),
        name=name,
    )(ctl, left, keys_values)


def norm_back_kernel(ctl_ref, parts_ref, pre_ref, gain_ref, out_ref):
    grad = jnp.sum(parts_ref[...].astype(F32), axis=0)
    tokens, width = grad.shape
    place = 1 - ctl_ref[3]
    half = LANES // 2
    lane = lax.broadcasted_iota(jnp.int32, (tokens, LANES), 1)
    blocks = pre_ref.shape[1] // 2

    def piece(block):
        high = pre_ref[:, block].astype(F32).reshape(tokens, LANES)
        low = pre_ref[:, blocks + block].astype(F32).reshape(tokens, LANES)
        held = high + low
        return jnp.where(place == block % 2, held, pltpu.roll(held, half, axis=1))

    for group in range(width // (2 * HEAD_DIM)):
        head = jnp.where(lane < half, piece(2 * group), piece(2 * group + 1))
        at = 2 * group * HEAD_DIM
        key_grad = grad[:, at : at + HEAD_DIM]
        factor = lax.rsqrt(jnp.mean(head * head, axis=-1, keepdims=True) + EPSILON)
        gained = gain_ref[...] * key_grad
        inner = jnp.mean(head * gained, axis=-1, keepdims=True)
        pre_grad = (factor * gained - factor * factor * factor * head * inner).astype(BF16)
        value_grad = grad[:, at + HEAD_DIM : at + 2 * HEAD_DIM].astype(BF16)
        for copy in range(out_ref.shape[0]):
            out_ref[copy, :, at : at + HEAD_DIM] = pre_grad
            out_ref[copy, :, at + HEAD_DIM : at + 2 * HEAD_DIM] = value_grad


def norm_back(ctl, parts, windows, gain, copies):
    tokens, width = parts.shape[1:]
    sources, rows, own, lanes = windows.shape
    last = lanes // LANES - 1
    return pl.pallas_call(
        norm_back_kernel,
        grid_spec=pltpu.PrefetchScalarGridSpec(
            num_scalar_prefetch=1,
            grid=(1,),
            in_specs=[
                whole(parts.shape),
                pl.BlockSpec(
                    (sources, rows, own, LANES), lambda i, ctl: (0, 0, 0, last * (1 - ctl[3]))
                ),
                whole(gain.shape),
            ],
            out_specs=whole((copies, tokens, width)),
        ),
        out_shape=jax.ShapeDtypeStruct((copies, tokens, width), BF16),
        compiler_params=params(1, SMALL_LIMIT),
        name="norm_back",
    )(ctl, parts, windows, gain)


def turn_kernel(ctl_ref, f_ref, out_ref):
    odd = ctl_ref[3]
    turned = f_ref[...].reshape(-1, f_ref.shape[-1]).T
    rows = out_ref.shape[0]
    spare = turned.shape[0] - rows

    @pl.when(odd == 0)
    def _():
        out_ref[...] = turned[:rows]

    @pl.when(odd != 0)
    def _():
        out_ref[...] = turned[spare:]


def turn(ctl, windows, feat):
    sources, rows, own, width = windows.shape
    tokens = sources * own
    return pl.pallas_call(
        turn_kernel,
        grid_spec=pltpu.PrefetchScalarGridSpec(
            num_scalar_prefetch=1,
            grid=(rows,),
            in_specs=[pl.BlockSpec((sources, 1, own, width), lambda r, ctl: (0, r, 0, 0))],
            out_specs=pl.BlockSpec((feat, tokens), lambda r, ctl: (0, r)),
        ),
        out_shape=jax.ShapeDtypeStruct((feat, rows * tokens), BF16),
        compiler_params=params(1, SMALL_LIMIT),
        name="turn",
    )(ctl, windows)


def weight_kernel(f_ref, g_ref, out_ref):
    out_ref[...] = jnp.dot(f_ref[...], g_ref[...], preferred_element_type=F32).astype(BF16)


def weight_grad(turned, grads):
    feat, tokens = turned.shape
    width = grads.shape[1]
    return pl.pallas_call(
        weight_kernel,
        out_shape=jax.ShapeDtypeStruct((feat, width), BF16),
        compiler_params=params(0, SMALL_LIMIT),
        cost_estimate=pl.CostEstimate(
            flops=2 * feat * tokens * width, bytes_accessed=2 * feat * tokens, transcendentals=0
        ),
        name="weight_grad",
    )(turned, grads)


def finish_kernel(parts_ref, key_ref, value_ref):
    total = jnp.sum(parts_ref[...].astype(F32), axis=0)
    for group in range(total.shape[1] // (2 * HEAD_DIM)):
        cols = slice(group * HEAD_DIM, (group + 1) * HEAD_DIM)
        at = 2 * group * HEAD_DIM
        key_ref[:, cols] = total[:, at : at + HEAD_DIM]
        value_ref[:, cols] = total[:, at + HEAD_DIM : at + 2 * HEAD_DIM]


def finish(parts):
    out = jax.ShapeDtypeStruct((parts.shape[1], parts.shape[2] // 2), F32)
    return pl.pallas_call(
        finish_kernel,
        out_shape=[out, out],
        compiler_params=params(0, SMALL_LIMIT),
        name="finish",
    )(parts)


def exchange(array, axes):
    return lax.all_to_all(array, axes, split_axis=0, concat_axis=0, tiled=True)


def on_device(queries, features, w_key, w_value, key_gain, out_grad, tile_counts, text_start):
    dp, seq = lax.axis_size("dp"), lax.axis_size("seq")
    rows, own, feat = features.shape
    text_dev = queries.shape[1]
    pairs = 2 * w_key.shape[1]
    tokens = rows * own
    gain = key_gain.reshape(1, HEAD_DIM)
    dp_index, seq_index = lax.axis_index("dp"), lax.axis_index("seq")
    ctl = jnp.stack([tile_counts[0], seq_index * text_dev, text_start[0], dp_index & 1])
    feats = features.reshape(tokens, feat)
    send, key_pre = project(feats, w_key, w_value, gain, seq)
    windows = cut(feats, key_pre, dp)
    arrived = exchange(send.reshape(seq * dp, own, pairs), ("seq", "dp"))
    windows, arrived, ctl = lax.optimization_barrier((windows, arrived, ctl))
    keys_values = arrived.reshape(seq * tokens, pairs)
    windows = exchange(windows, "dp").reshape(dp, rows, own, -1)
    probs, score_grads, grads = attend(ctl, queries[0], out_grad[0], keys_values)
    grads, windows = lax.optimization_barrier((grads, windows))
    shares = exchange(grads.reshape(seq, tokens, pairs), "seq")
    attended = apply(ctl, probs, keys_values, text_dev, HEAD_DIM, True, "attended")
    shares, attended = lax.optimization_barrier((shares, attended))
    rounded = norm_back(ctl, shares, windows, gain, dp)
    everywhere = exchange(rounded, "dp").reshape(dp * tokens, pairs)
    turned = turn(ctl, windows, feat // dp)
    query_grad = apply(ctl, score_grads, keys_values, text_dev, 0, False, "query_grad")
    everywhere, query_grad = lax.optimization_barrier((everywhere, query_grad))
    partial = weight_grad(turned, everywhere)
    pieces = exchange(partial.reshape(seq, feat // dp // seq, pairs), "seq")
    key_weight, value_weight = finish(pieces)
    return attended[None], query_grad[None], key_weight, value_weight


def solution(mesh):
    placed = (
        P("dp", "seq", "mp"),
        P(None, ("seq", "dp"), None),
        P(None, "mp"),
        P(None, "mp"),
        P(),
        P("dp", "seq", "mp"),
        P("dp"),
        P("dp"),
    )
    return jax.shard_map(
        on_device,
        mesh=mesh,
        in_specs=placed,
        out_specs=(
            P("dp", "seq", "mp"),
            P("dp", "seq", "mp"),
            P(("dp", "seq"), "mp"),
            P(("dp", "seq"), "mp"),
        ),
        check_vma=False,
    )
```

```python
import functools

import jax
import jax.numpy as jnp
from jax import lax
from jax.experimental import pallas as pl
from jax.experimental.pallas import tpu as pltpu
from jax.sharding import PartitionSpec as P

HEAD_DIM = 128
TILES = 4
EPSILON = 1e-05
SCALE = HEAD_DIM**-0.5
EXP2_SCALE = SCALE * 1.4426950408889634
BF16 = jnp.bfloat16
F32 = jnp.float32
LANES = 128
SUBLANES = 8
CHUNK = 128
VMEM_LIMIT = 59 * 2**20
SMALL_LIMIT = 16 * 2**20

NN = (((1,), (0,)), ((), ()))
NT = (((1,), (1,)), ((), ()))


def whole(shape):
    return pl.BlockSpec(shape, lambda *_: (0,) * len(shape))


def params(axes, limit=VMEM_LIMIT):
    return pltpu.CompilerParams(
        vmem_limit_bytes=limit, dimension_semantics=("arbitrary",) * axes
    )


def project_kernel(
    f_hbm, wk_hbm, wv_hbm, gain_ref, send_ref, pre_ref, f_ref, wk_ref, wv_ref, arrived, *, parts
):
    tokens, feat = f_ref.shape
    kv_dim = wk_ref.shape[1]
    depth = feat // parts
    copies = []
    for part in range(parts):
        here = pl.ds(part * depth, depth)
        copies.append(
            [
                pltpu.make_async_copy(f_hbm.at[:, here], f_ref.at[:, here], arrived.at[0, part]),
                pltpu.make_async_copy(wk_hbm.at[here], wk_ref.at[here], arrived.at[1, part]),
                pltpu.make_async_copy(wv_hbm.at[here], wv_ref.at[here], arrived.at[2, part]),
            ]
        )
    for trio in copies:
        for copy in trio:
            copy.start()
    keys = jnp.zeros((tokens, kv_dim), F32)
    values = jnp.zeros((tokens, kv_dim), F32)
    for part, trio in enumerate(copies):
        here = slice(part * depth, (part + 1) * depth)
        for copy in trio:
            copy.wait()
        left = f_ref[:, here]
        keys += jnp.dot(left, wk_ref[here], preferred_element_type=F32)
        values += jnp.dot(left, wv_ref[here], preferred_element_type=F32)
    pre_ref[...] = keys
    for group in range(kv_dim // HEAD_DIM):
        cols = slice(group * HEAD_DIM, (group + 1) * HEAD_DIM)
        head = keys[:, cols]
        factor = lax.rsqrt(jnp.mean(head * head, axis=-1, keepdims=True) + EPSILON)
        key = (head * factor * gain_ref[...]).astype(BF16)
        value = values[:, cols].astype(BF16)
        at = 2 * group * HEAD_DIM
        for copy in range(send_ref.shape[0]):
            send_ref[copy, :, at : at + HEAD_DIM] = key
            send_ref[copy, :, at + HEAD_DIM : at + 2 * HEAD_DIM] = value


def project(feats, w_key, w_value, gain, copies):
    tokens, feat = feats.shape
    kv_dim = w_key.shape[1]
    parts = 6
    send, pre = (copies, tokens, 2 * kv_dim), (tokens, kv_dim)
    anywhere = pl.BlockSpec(memory_space=pl.ANY)
    return pl.pallas_call(
        functools.partial(project_kernel, parts=parts),
        in_specs=[anywhere, anywhere, anywhere, pl.BlockSpec(memory_space=pltpu.VMEM)],
        out_shape=[jax.ShapeDtypeStruct(send, BF16), jax.ShapeDtypeStruct(pre, F32)],
        scratch_shapes=[
            pltpu.VMEM((tokens, feat), BF16),
            pltpu.VMEM((feat, kv_dim), BF16),
            pltpu.VMEM((feat, kv_dim), BF16),
            pltpu.SemaphoreType.DMA((3, parts)),
        ],
        compiler_params=params(0),
        cost_estimate=pl.CostEstimate(
            flops=4 * tokens * feat * kv_dim,
            bytes_accessed=4 * feat * kv_dim + 4 * tokens * feat,
            transcendentals=0,
        ),
        name="project",
    )(feats, w_key, w_value, gain)


def cut_kernel(f_ref, pre_ref, win_ref):
    windows, tokens, width = win_ref.shape
    tiles = f_ref.shape[1] // LANES
    own = tokens // windows
    half = LANES // 2
    lane = lax.broadcasted_iota(jnp.int32, (own, LANES), 1)
    for window in range(windows):
        tile = window * tiles // windows
        win_ref[window] = f_ref[:, tile * LANES : tile * LANES + width]
        head = pre_ref[window * own : (window + 1) * own]
        high = head.astype(BF16).astype(F32)
        pair = jnp.concatenate([high, head - high], axis=1)
        place = 1 - window % 2
        at = (width - LANES) * place
        for block in range(windows):
            piece = pair[:, block // 2 * LANES : (block // 2 + 1) * LANES]
            if block % 2 != place:
                piece = pltpu.roll(piece, half, axis=1)
            rows = slice(block * own, (block + 1) * own)
            kept = win_ref[window, rows, at : at + LANES].astype(F32)
            mixed = jnp.where((lane >= half) == bool(place), piece, kept)
            win_ref[window, rows, at : at + LANES] = mixed.astype(BF16)


def cut(feats, key_pre, windows):
    tokens, feat = feats.shape
    width = -(-(feat // windows) // LANES) * LANES
    return pl.pallas_call(
        cut_kernel,
        out_shape=jax.ShapeDtypeStruct((windows, tokens, width), BF16),
        compiler_params=params(0, SMALL_LIMIT),
        cost_estimate=pl.CostEstimate(
            flops=0, bytes_accessed=6 * tokens * feat, transcendentals=0
        ),
        name="cut",
    )(feats, key_pre)


def attend_kernel(
    ctl_ref, q_ref, d_ref, kv_ref, prob_ref, grad_ref, dkv_ref, dk_sum, dv_sum, powers_ref, live_ref, *, heads
):
    step, steps = pl.program_id(1), pl.num_programs(1)
    rows = q_ref.shape[0]
    img = kv_ref.shape[0]

    @pl.when(step == 0)
    def _():
        dk_sum[...] = jnp.zeros_like(dk_sum)
        dv_sum[...] = jnp.zeros_like(dv_sum)

    def run(length):
        position = ctl_ref[1] + lax.broadcasted_iota(jnp.int32, (rows, HEAD_DIM), 0)
        live = position >= ctl_ref[2]
        chunks = [slice(at, at + CHUNK) for at in range(0, length, CHUNK)]
        folded = (CHUNK // SUBLANES, SUBLANES, rows)

        def against(chunk, start, other):
            left = kv_ref[chunk, start : start + HEAD_DIM]
            out = lax.dot_general(left, other, NT, preferred_element_type=F32)
            return out.reshape(folded)

        def first(head):
            cols = slice(head * HEAD_DIM, (head + 1) * HEAD_DIM)
            here = slice(head * rows, (head + 1) * rows)
            query = q_ref[:, cols]
            cotangent = jnp.where(live, d_ref[:, cols], jnp.zeros((), BF16))
            live_ref[here] = cotangent
            tops, sums, deltas = [], [], []
            for chunk in chunks:
                scores = against(chunk, 0, query)
                top = jnp.max(scores, axis=0)
                powers = jnp.exp2((scores - top[None]) * EXP2_SCALE)
                powers_ref[chunk, here] = powers.reshape(CHUNK, rows)
                tops.append(top)
                sums.append(jnp.sum(powers, axis=0))
                deltas.append(jnp.sum(powers * against(chunk, HEAD_DIM, cotangent), axis=0))
            row_max = jnp.max(functools.reduce(jnp.maximum, tops), axis=0, keepdims=True)
            factors = [jnp.exp2((top - row_max) * EXP2_SCALE) for top in tops]

            def over_rows(parts):
                total = sum(part * factor for part, factor in zip(parts, factors))
                return jnp.sum(total, axis=0, keepdims=True)

            inverse = 1.0 / over_rows(sums)
            delta = over_rows(deltas) * inverse
            return cotangent, here, [factor * inverse for factor in factors], delta

        def second(cotangent, here, factors, delta):
            for chunk, factor in zip(chunks, factors):
                prob = powers_ref[chunk, here].reshape(folded) * factor[None]
                prob_ref[chunk, here] = prob.reshape(CHUNK, rows).astype(BF16)
                score_grad = prob * (against(chunk, HEAD_DIM, cotangent) - delta[None])
                grad_ref[chunk, here] = score_grad.reshape(CHUNK, rows).astype(BF16)

        held = first(0)
        for head in range(heads):
            ahead = first(head + 1) if head + 1 < heads else None
            second(*held)
            held = ahead
        queries = jnp.concatenate(
            [q_ref[:, head * HEAD_DIM : (head + 1) * HEAD_DIM] for head in range(heads)], axis=0
        )
        dk_sum[:length] += jnp.dot(grad_ref[:length], queries, preferred_element_type=F32)
        dv_sum[:length] += jnp.dot(prob_ref[:length], live_ref[...], preferred_element_type=F32)

    for count in range(1, TILES + 1):
        pl.when(ctl_ref[0] == count)(functools.partial(run, count * (img // TILES)))

    @pl.when(step == steps - 1)
    def _():
        dkv_ref[:, :HEAD_DIM] = (dk_sum[...] * SCALE).astype(BF16)
        dkv_ref[:, HEAD_DIM:] = dv_sum[...].astype(BF16)


def attend(ctl, queries, out_grad, keys_values):
    rows, width = queries.shape
    img, pairs = keys_values.shape
    groups = pairs // (2 * HEAD_DIM)
    heads = 2
    steps = width // groups // HEAD_DIM // heads
    cols = pl.BlockSpec((rows, heads * HEAD_DIM), lambda g, h, ctl: (0, g * steps + h))
    pair = pl.BlockSpec((img, 2 * HEAD_DIM), lambda g, h, ctl: (0, g))
    square = pl.BlockSpec((img, heads * rows), lambda g, h, ctl: (0, g * steps + h))
    big = jax.ShapeDtypeStruct((img, width // HEAD_DIM * rows), BF16)
    return pl.pallas_call(
        functools.partial(attend_kernel, heads=heads),
        grid_spec=pltpu.PrefetchScalarGridSpec(
            num_scalar_prefetch=1,
            grid=(groups, steps),
            in_specs=[cols, cols, pair],
            out_specs=[square, square, pair],
            scratch_shapes=[pltpu.VMEM((img, HEAD_DIM), F32)] * 2
            + [
                pltpu.VMEM((img, heads * rows), F32),
                pltpu.VMEM((heads * rows, HEAD_DIM), BF16),
            ],
        ),
        out_shape=[big, big, jax.ShapeDtypeStruct((img, pairs), BF16)],
        compiler_params=params(2),
        cost_estimate=pl.CostEstimate(
            flops=20 * rows * width * img, bytes_accessed=8 * rows * width, transcendentals=0
        ),
        name="attend",
    )(ctl, queries, out_grad, keys_values)


def apply_kernel(ctl_ref, left_ref, kv_ref, out_ref, turned_ref, *, heads, start, masked):
    rows = out_ref.shape[0]
    img = kv_ref.shape[0]

    @pl.when(pl.program_id(1) == 0)
    def _():
        turned_ref[...] = kv_ref[:, start : start + HEAD_DIM].T

    def run(length):
        position = ctl_ref[1] + lax.broadcasted_iota(jnp.int32, (rows, HEAD_DIM), 0)
        live = position >= ctl_ref[2]
        for head in range(heads):
            left = left_ref[:length, head * rows : (head + 1) * rows]
            out = jnp.dot(turned_ref[:, :length], left, preferred_element_type=F32).T
            out = jnp.where(live, out, 0.0) if masked else out * SCALE
            out_ref[:, head * HEAD_DIM : (head + 1) * HEAD_DIM] = out.astype(BF16)

    for count in range(1, TILES + 1):
        pl.when(ctl_ref[0] == count)(functools.partial(run, count * (img // TILES)))


def apply(ctl, left, keys_values, rows, start, masked, name):
    img, pairs = keys_values.shape
    groups = pairs // (2 * HEAD_DIM)
    heads = 2
    all_heads = left.shape[1] // rows
    steps = all_heads // groups // heads
    return pl.pallas_call(
        functools.partial(apply_kernel, heads=heads, start=start, masked=masked),
        grid_spec=pltpu.PrefetchScalarGridSpec(
            num_scalar_prefetch=1,
            grid=(groups, steps),
            in_specs=[
                pl.BlockSpec((img, heads * rows), lambda g, h, ctl: (0, g * steps + h)),
                pl.BlockSpec((img, 2 * HEAD_DIM), lambda g, h, ctl: (0, g)),
            ],
            out_specs=pl.BlockSpec((rows, heads * HEAD_DIM), lambda g, h, ctl: (0, g * steps + h)),
            scratch_shapes=[pltpu.VMEM((HEAD_DIM, img), BF16)],
        ),
        out_shape=jax.ShapeDtypeStruct((rows, all_heads * HEAD_DIM), BF16),
        compiler_params=params(2),
        cost_estimate=pl.CostEstimate(
            flops=2 * img * rows * all_heads * HEAD_DIM,
            bytes_accessed=2 * img * rows * all_heads,
            transcendentals=0,
        ),
        name=name,
    )(ctl, left, keys_values)


def norm_back_kernel(ctl_ref, parts_ref, pre_ref, gain_ref, out_ref):
    grad = jnp.sum(parts_ref[...].astype(F32), axis=0)
    tokens, width = grad.shape
    place = 1 - ctl_ref[3]
    half = LANES // 2
    lane = lax.broadcasted_iota(jnp.int32, (tokens, LANES), 1)
    blocks = pre_ref.shape[1] // 2

    def piece(block):
        high = pre_ref[:, block].astype(F32).reshape(tokens, LANES)
        low = pre_ref[:, blocks + block].astype(F32).reshape(tokens, LANES)
        held = high + low
        return jnp.where(place == block % 2, held, pltpu.roll(held, half, axis=1))

    for group in range(width // (2 * HEAD_DIM)):
        head = jnp.where(lane < half, piece(2 * group), piece(2 * group + 1))
        at = 2 * group * HEAD_DIM
        key_grad = grad[:, at : at + HEAD_DIM]
        factor = lax.rsqrt(jnp.mean(head * head, axis=-1, keepdims=True) + EPSILON)
        gained = gain_ref[...] * key_grad
        inner = jnp.mean(head * gained, axis=-1, keepdims=True)
        pre_grad = (factor * gained - factor * factor * factor * head * inner).astype(BF16)
        value_grad = grad[:, at + HEAD_DIM : at + 2 * HEAD_DIM].astype(BF16)
        out_ref[:, at : at + HEAD_DIM] = pre_grad
        out_ref[:, at + HEAD_DIM : at + 2 * HEAD_DIM] = value_grad


def norm_back(ctl, parts, windows, gain):
    tokens, width = parts.shape[1:]
    sources, rows, own, lanes = windows.shape
    last = lanes // LANES - 1
    return pl.pallas_call(
        norm_back_kernel,
        grid_spec=pltpu.PrefetchScalarGridSpec(
            num_scalar_prefetch=1,
            grid=(1,),
            in_specs=[
                whole(parts.shape),
                pl.BlockSpec(
                    (sources, rows, own, LANES), lambda i, ctl: (0, 0, 0, last * (1 - ctl[3]))
                ),
                whole(gain.shape),
            ],
            out_specs=whole((tokens, width)),
        ),
        out_shape=jax.ShapeDtypeStruct((tokens, width), BF16),
        compiler_params=params(1, SMALL_LIMIT),
        name="norm_back",
    )(ctl, parts, windows, gain)


def turn_kernel(ctl_ref, f_ref, out_ref):
    odd = ctl_ref[3]
    turned = f_ref[...].reshape(-1, f_ref.shape[-1]).T
    rows = out_ref.shape[0]
    spare = turned.shape[0] - rows

    @pl.when(odd == 0)
    def _():
        out_ref[...] = turned[:rows]

    @pl.when(odd != 0)
    def _():
        out_ref[...] = turned[spare:]


def turn(ctl, windows, feat):
    sources, rows, own, width = windows.shape
    tokens = sources * own
    return pl.pallas_call(
        turn_kernel,
        grid_spec=pltpu.PrefetchScalarGridSpec(
            num_scalar_prefetch=1,
            grid=(rows,),
            in_specs=[pl.BlockSpec((sources, 1, own, width), lambda r, ctl: (0, r, 0, 0))],
            out_specs=pl.BlockSpec((feat, tokens), lambda r, ctl: (0, r)),
        ),
        out_shape=jax.ShapeDtypeStruct((feat, rows * tokens), BF16),
        compiler_params=params(1, SMALL_LIMIT),
        name="turn",
    )(ctl, windows)


def weight_kernel(ctl_ref, f_ref, *refs):
    pieces, (out_ref, grads_ref) = refs[:-2], refs[-2:]
    tokens = pieces[0].shape[0]
    for away, piece in enumerate(pieces):
        source = lax.rem(ctl_ref[4] + len(pieces) - away, len(pieces))
        grads_ref[pl.ds(pl.multiple_of(source * tokens, tokens), tokens)] = piece[...]
    out_ref[...] = jnp.dot(f_ref[...], grads_ref[...], preferred_element_type=F32).astype(BF16)


def weight_grad(ctl, turned, pieces):
    feat, tokens = turned.shape
    width = pieces[0].shape[1]
    return pl.pallas_call(
        weight_kernel,
        grid_spec=pltpu.PrefetchScalarGridSpec(
            num_scalar_prefetch=1,
            grid=(1,),
            in_specs=[whole(turned.shape)] + [whole(piece.shape) for piece in pieces],
            out_specs=whole((feat, width)),
            scratch_shapes=[pltpu.VMEM((tokens, width), BF16)],
        ),
        out_shape=jax.ShapeDtypeStruct((feat, width), BF16),
        compiler_params=params(1, SMALL_LIMIT),
        cost_estimate=pl.CostEstimate(
            flops=2 * feat * tokens * width, bytes_accessed=2 * feat * tokens, transcendentals=0
        ),
        name="weight_grad",
    )(ctl, turned, *pieces)


def finish_kernel(parts_ref, key_ref, value_ref):
    total = jnp.sum(parts_ref[...].astype(F32), axis=0)
    for group in range(total.shape[1] // (2 * HEAD_DIM)):
        cols = slice(group * HEAD_DIM, (group + 1) * HEAD_DIM)
        at = 2 * group * HEAD_DIM
        key_ref[:, cols] = total[:, at : at + HEAD_DIM]
        value_ref[:, cols] = total[:, at + HEAD_DIM : at + 2 * HEAD_DIM]


def finish(parts):
    out = jax.ShapeDtypeStruct((parts.shape[1], parts.shape[2] // 2), F32)
    return pl.pallas_call(
        finish_kernel,
        out_shape=[out, out],
        compiler_params=params(0, SMALL_LIMIT),
        name="finish",
    )(parts)


def exchange(array, axes):
    return lax.all_to_all(array, axes, split_axis=0, concat_axis=0, tiled=True)


def on_device(queries, features, w_key, w_value, key_gain, out_grad, tile_counts, text_start):
    dp, seq = lax.axis_size("dp"), lax.axis_size("seq")
    rows, own, feat = features.shape
    text_dev = queries.shape[1]
    pairs = 2 * w_key.shape[1]
    tokens = rows * own
    gain = key_gain.reshape(1, HEAD_DIM)
    dp_index, seq_index = lax.axis_index("dp"), lax.axis_index("seq")
    ctl = jnp.stack(
        [tile_counts[0], seq_index * text_dev, text_start[0], dp_index & 1, dp_index]
    )
    feats = features.reshape(tokens, feat)
    send, key_pre = project(feats, w_key, w_value, gain, seq)
    windows = cut(feats, key_pre, dp)
    arrived = exchange(send.reshape(seq * dp, own, pairs), ("seq", "dp"))
    windows, arrived, ctl = lax.optimization_barrier((windows, arrived, ctl))
    keys_values = arrived.reshape(seq * tokens, pairs)
    windows = exchange(windows, "dp").reshape(dp, rows, own, -1)
    probs, score_grads, grads = attend(ctl, queries[0], out_grad[0], keys_values)
    grads, windows = lax.optimization_barrier((grads, windows))
    shares = exchange(grads.reshape(seq, tokens, pairs), "seq")
    attended = apply(ctl, probs, keys_values, text_dev, HEAD_DIM, True, "attended")
    shares, attended = lax.optimization_barrier((shares, attended))
    rounded = norm_back(ctl, shares, windows, gain)
    everywhere = [rounded]
    for away in range(1, dp):
        to = [(source, (source + away) % dp) for source in range(dp)]
        everywhere.append(lax.ppermute(rounded, "dp", to))
    turned = turn(ctl, windows, feat // dp)
    partial = weight_grad(ctl, turned, everywhere)
    pieces = exchange(partial.reshape(seq, feat // dp // seq, pairs), "seq")
    query_grad = apply(ctl, score_grads, keys_values, text_dev, 0, False, "query_grad")
    pieces, query_grad = lax.optimization_barrier((pieces, query_grad))
    key_weight, value_weight = finish(pieces)
    return attended[None], query_grad[None], key_weight, value_weight


def solution(mesh):
    placed = (
        P("dp", "seq", "mp"),
        P(None, ("seq", "dp"), None),
        P(None, "mp"),
        P(None, "mp"),
        P(),
        P("dp", "seq", "mp"),
        P("dp"),
        P("dp"),
    )
    return jax.shard_map(
        on_device,
        mesh=mesh,
        in_specs=placed,
        out_specs=(
            P("dp", "seq", "mp"),
            P("dp", "seq", "mp"),
            P(("dp", "seq"), "mp"),
            P(("dp", "seq"), "mp"),
        ),
        check_vma=False,
    )
```

```python
import functools

import jax
import jax.numpy as jnp
from jax import lax
from jax.experimental import pallas as pl
from jax.experimental.pallas import tpu as pltpu
from jax.sharding import PartitionSpec as P

HEAD_DIM = 128
TILES = 4
EPSILON = 1e-05
SCALE = HEAD_DIM**-0.5
EXP2_SCALE = SCALE * 1.4426950408889634
BF16 = jnp.bfloat16
F32 = jnp.float32
LANES = 128
SUBLANES = 8
CHUNK = 128
VMEM_LIMIT = 59 * 2**20
SMALL_LIMIT = 16 * 2**20

NN = (((1,), (0,)), ((), ()))
NT = (((1,), (1,)), ((), ()))


def whole(shape):
    return pl.BlockSpec(shape, lambda *_: (0,) * len(shape))


def params(axes, limit=VMEM_LIMIT):
    return pltpu.CompilerParams(
        vmem_limit_bytes=limit, dimension_semantics=("arbitrary",) * axes
    )


def project_kernel(
    f_hbm, wk_hbm, wv_hbm, gain_ref, send_ref, pre_ref, f_ref, wk_ref, wv_ref, arrived, *, parts
):
    tokens, feat = f_ref.shape
    kv_dim = wk_ref.shape[1]
    depth = feat // parts
    copies = []
    for part in range(parts):
        here = pl.ds(part * depth, depth)
        copies.append(
            [
                pltpu.make_async_copy(f_hbm.at[:, here], f_ref.at[:, here], arrived.at[0, part]),
                pltpu.make_async_copy(wk_hbm.at[here], wk_ref.at[here], arrived.at[1, part]),
                pltpu.make_async_copy(wv_hbm.at[here], wv_ref.at[here], arrived.at[2, part]),
            ]
        )
    for trio in copies:
        for copy in trio:
            copy.start()
    keys = jnp.zeros((tokens, kv_dim), F32)
    values = jnp.zeros((tokens, kv_dim), F32)
    for part, trio in enumerate(copies):
        here = slice(part * depth, (part + 1) * depth)
        for copy in trio:
            copy.wait()
        left = f_ref[:, here]
        keys += jnp.dot(left, wk_ref[here], preferred_element_type=F32)
        values += jnp.dot(left, wv_ref[here], preferred_element_type=F32)
    pre_ref[...] = keys
    for group in range(kv_dim // HEAD_DIM):
        cols = slice(group * HEAD_DIM, (group + 1) * HEAD_DIM)
        head = keys[:, cols]
        factor = lax.rsqrt(jnp.mean(head * head, axis=-1, keepdims=True) + EPSILON)
        key = (head * factor * gain_ref[...]).astype(BF16)
        value = values[:, cols].astype(BF16)
        at = 2 * group * HEAD_DIM
        for copy in range(send_ref.shape[0]):
            send_ref[copy, :, at : at + HEAD_DIM] = key
            send_ref[copy, :, at + HEAD_DIM : at + 2 * HEAD_DIM] = value


def project(feats, w_key, w_value, gain, copies):
    tokens, feat = feats.shape
    kv_dim = w_key.shape[1]
    parts = 6
    send, pre = (copies, tokens, 2 * kv_dim), (tokens, kv_dim)
    anywhere = pl.BlockSpec(memory_space=pl.ANY)
    return pl.pallas_call(
        functools.partial(project_kernel, parts=parts),
        in_specs=[anywhere, anywhere, anywhere, pl.BlockSpec(memory_space=pltpu.VMEM)],
        out_shape=[jax.ShapeDtypeStruct(send, BF16), jax.ShapeDtypeStruct(pre, F32)],
        scratch_shapes=[
            pltpu.VMEM((tokens, feat), BF16),
            pltpu.VMEM((feat, kv_dim), BF16),
            pltpu.VMEM((feat, kv_dim), BF16),
            pltpu.SemaphoreType.DMA((3, parts)),
        ],
        compiler_params=params(0),
        cost_estimate=pl.CostEstimate(
            flops=4 * tokens * feat * kv_dim,
            bytes_accessed=4 * feat * kv_dim + 4 * tokens * feat,
            transcendentals=0,
        ),
        name="project",
    )(feats, w_key, w_value, gain)


def cut_kernel(f_ref, pre_ref, win_ref):
    windows, tokens, width = win_ref.shape
    tiles = f_ref.shape[1] // LANES
    own = tokens // windows
    half = LANES // 2
    lane = lax.broadcasted_iota(jnp.int32, (own, LANES), 1)
    for window in range(windows):
        tile = window * tiles // windows
        win_ref[window] = f_ref[:, tile * LANES : tile * LANES + width]
        head = pre_ref[window * own : (window + 1) * own]
        high = head.astype(BF16).astype(F32)
        pair = jnp.concatenate([high, head - high], axis=1)
        place = 1 - window % 2
        at = (width - LANES) * place
        for block in range(windows):
            piece = pair[:, block // 2 * LANES : (block // 2 + 1) * LANES]
            if block % 2 != place:
                piece = pltpu.roll(piece, half, axis=1)
            rows = slice(block * own, (block + 1) * own)
            kept = win_ref[window, rows, at : at + LANES].astype(F32)
            mixed = jnp.where((lane >= half) == bool(place), piece, kept)
            win_ref[window, rows, at : at + LANES] = mixed.astype(BF16)


def cut(feats, key_pre, windows):
    tokens, feat = feats.shape
    width = -(-(feat // windows) // LANES) * LANES
    return pl.pallas_call(
        cut_kernel,
        out_shape=jax.ShapeDtypeStruct((windows, tokens, width), BF16),
        compiler_params=params(0, SMALL_LIMIT),
        cost_estimate=pl.CostEstimate(
            flops=0, bytes_accessed=6 * tokens * feat, transcendentals=0
        ),
        name="cut",
    )(feats, key_pre)


def attend_kernel(
    ctl_ref, q_ref, d_ref, kv_ref, prob_ref, grad_ref, dkv_ref, dk_sum, dv_sum, powers_ref, live_ref, *, heads
):
    step, steps = pl.program_id(1), pl.num_programs(1)
    rows = q_ref.shape[0]
    img = kv_ref.shape[0]

    @pl.when(step == 0)
    def _():
        dk_sum[...] = jnp.zeros_like(dk_sum)
        dv_sum[...] = jnp.zeros_like(dv_sum)

    def run(length):
        position = ctl_ref[1] + lax.broadcasted_iota(jnp.int32, (rows, HEAD_DIM), 0)
        live = position >= ctl_ref[2]
        chunks = [slice(at, at + CHUNK) for at in range(0, length, CHUNK)]
        folded = (CHUNK // SUBLANES, SUBLANES, rows)

        def against(chunk, start, other):
            left = kv_ref[chunk, start : start + HEAD_DIM]
            out = lax.dot_general(left, other, NT, preferred_element_type=F32)
            return out.reshape(folded)

        def first(head):
            cols = slice(head * HEAD_DIM, (head + 1) * HEAD_DIM)
            here = slice(head * rows, (head + 1) * rows)
            query = q_ref[:, cols]
            cotangent = jnp.where(live, d_ref[:, cols], jnp.zeros((), BF16))
            live_ref[here] = cotangent
            tops, sums, deltas = [], [], []
            for chunk in chunks:
                scores = against(chunk, 0, query)
                top = jnp.max(scores, axis=0)
                powers = jnp.exp2((scores - top[None]) * EXP2_SCALE)
                powers_ref[chunk, here] = powers.reshape(CHUNK, rows)
                tops.append(top)
                sums.append(jnp.sum(powers, axis=0))
                deltas.append(jnp.sum(powers * against(chunk, HEAD_DIM, cotangent), axis=0))
            row_max = jnp.max(functools.reduce(jnp.maximum, tops), axis=0, keepdims=True)
            factors = [jnp.exp2((top - row_max) * EXP2_SCALE) for top in tops]

            def over_rows(parts):
                total = sum(part * factor for part, factor in zip(parts, factors))
                return jnp.sum(total, axis=0, keepdims=True)

            inverse = 1.0 / over_rows(sums)
            delta = over_rows(deltas) * inverse
            return cotangent, here, [factor * inverse for factor in factors], delta

        def second(cotangent, here, factors, delta):
            for chunk, factor in zip(chunks, factors):
                prob = powers_ref[chunk, here].reshape(folded) * factor[None]
                prob_ref[chunk, here] = prob.reshape(CHUNK, rows).astype(BF16)
                score_grad = prob * (against(chunk, HEAD_DIM, cotangent) - delta[None])
                grad_ref[chunk, here] = score_grad.reshape(CHUNK, rows).astype(BF16)

        held = first(0)
        for head in range(heads):
            ahead = first(head + 1) if head + 1 < heads else None
            second(*held)
            held = ahead
        queries = jnp.concatenate(
            [q_ref[:, head * HEAD_DIM : (head + 1) * HEAD_DIM] for head in range(heads)], axis=0
        )
        dk_sum[:length] += jnp.dot(grad_ref[:length], queries, preferred_element_type=F32)
        dv_sum[:length] += jnp.dot(prob_ref[:length], live_ref[...], preferred_element_type=F32)

    for count in range(1, TILES + 1):
        pl.when(ctl_ref[0] == count)(functools.partial(run, count * (img // TILES)))

    @pl.when(step == steps - 1)
    def _():
        dkv_ref[:, :HEAD_DIM] = (dk_sum[...] * SCALE).astype(BF16)
        dkv_ref[:, HEAD_DIM:] = dv_sum[...].astype(BF16)


def attend(ctl, queries, out_grad, keys_values):
    rows, width = queries.shape
    img, pairs = keys_values.shape
    groups = pairs // (2 * HEAD_DIM)
    heads = 2
    steps = width // groups // HEAD_DIM // heads
    cols = pl.BlockSpec((rows, heads * HEAD_DIM), lambda g, h, ctl: (0, g * steps + h))
    pair = pl.BlockSpec((img, 2 * HEAD_DIM), lambda g, h, ctl: (0, g))
    square = pl.BlockSpec((img, heads * rows), lambda g, h, ctl: (0, g * steps + h))
    big = jax.ShapeDtypeStruct((img, width // HEAD_DIM * rows), BF16)
    return pl.pallas_call(
        functools.partial(attend_kernel, heads=heads),
        grid_spec=pltpu.PrefetchScalarGridSpec(
            num_scalar_prefetch=1,
            grid=(groups, steps),
            in_specs=[cols, cols, pair],
            out_specs=[square, square, pair],
            scratch_shapes=[pltpu.VMEM((img, HEAD_DIM), F32)] * 2
            + [
                pltpu.VMEM((img, heads * rows), F32),
                pltpu.VMEM((heads * rows, HEAD_DIM), BF16),
            ],
        ),
        out_shape=[big, big, jax.ShapeDtypeStruct((img, pairs), BF16)],
        compiler_params=params(2),
        cost_estimate=pl.CostEstimate(
            flops=20 * rows * width * img, bytes_accessed=8 * rows * width, transcendentals=0
        ),
        name="attend",
    )(ctl, queries, out_grad, keys_values)


def apply_kernel(ctl_ref, left_ref, kv_ref, out_ref, turned_ref, *, heads, start, masked):
    rows = out_ref.shape[0]
    img = kv_ref.shape[0]

    @pl.when(pl.program_id(1) == 0)
    def _():
        turned_ref[...] = kv_ref[:, start : start + HEAD_DIM].T

    def run(length):
        position = ctl_ref[1] + lax.broadcasted_iota(jnp.int32, (rows, HEAD_DIM), 0)
        live = position >= ctl_ref[2]
        for head in range(heads):
            left = left_ref[:length, head * rows : (head + 1) * rows]
            out = jnp.dot(turned_ref[:, :length], left, preferred_element_type=F32).T
            out = jnp.where(live, out, 0.0) if masked else out * SCALE
            out_ref[:, head * HEAD_DIM : (head + 1) * HEAD_DIM] = out.astype(BF16)

    for count in range(1, TILES + 1):
        pl.when(ctl_ref[0] == count)(functools.partial(run, count * (img // TILES)))


def apply(ctl, left, keys_values, rows, start, masked, name):
    img, pairs = keys_values.shape
    groups = pairs // (2 * HEAD_DIM)
    heads = 4
    all_heads = left.shape[1] // rows
    steps = all_heads // groups // heads
    return pl.pallas_call(
        functools.partial(apply_kernel, heads=heads, start=start, masked=masked),
        grid_spec=pltpu.PrefetchScalarGridSpec(
            num_scalar_prefetch=1,
            grid=(groups, steps),
            in_specs=[
                pl.BlockSpec((img, heads * rows), lambda g, h, ctl: (0, g * steps + h)),
                pl.BlockSpec((img, 2 * HEAD_DIM), lambda g, h, ctl: (0, g)),
            ],
            out_specs=pl.BlockSpec((rows, heads * HEAD_DIM), lambda g, h, ctl: (0, g * steps + h)),
            scratch_shapes=[pltpu.VMEM((HEAD_DIM, img), BF16)],
        ),
        out_shape=jax.ShapeDtypeStruct((rows, all_heads * HEAD_DIM), BF16),
        compiler_params=params(2),
        cost_estimate=pl.CostEstimate(
            flops=2 * img * rows * all_heads * HEAD_DIM,
            bytes_accessed=2 * img * rows * all_heads,
            transcendentals=0,
        ),
        name=name,
    )(ctl, left, keys_values)


def norm_back_kernel(ctl_ref, parts_ref, pre_ref, gain_ref, out_ref):
    grad = jnp.sum(parts_ref[...].astype(F32), axis=0)
    tokens, width = grad.shape
    place = 1 - ctl_ref[3]
    half = LANES // 2
    lane = lax.broadcasted_iota(jnp.int32, (tokens, LANES), 1)
    blocks = pre_ref.shape[1] // 2

    def piece(block):
        high = pre_ref[:, block].astype(F32).reshape(tokens, LANES)
        low = pre_ref[:, blocks + block].astype(F32).reshape(tokens, LANES)
        held = high + low
        return jnp.where(place == block % 2, held, pltpu.roll(held, half, axis=1))

    for group in range(width // (2 * HEAD_DIM)):
        head = jnp.where(lane < half, piece(2 * group), piece(2 * group + 1))
        at = 2 * group * HEAD_DIM
        key_grad = grad[:, at : at + HEAD_DIM]
        factor = lax.rsqrt(jnp.mean(head * head, axis=-1, keepdims=True) + EPSILON)
        gained = gain_ref[...] * key_grad
        inner = jnp.mean(head * gained, axis=-1, keepdims=True)
        pre_grad = (factor * gained - factor * factor * factor * head * inner).astype(BF16)
        value_grad = grad[:, at + HEAD_DIM : at + 2 * HEAD_DIM].astype(BF16)
        out_ref[:, at : at + HEAD_DIM] = pre_grad
        out_ref[:, at + HEAD_DIM : at + 2 * HEAD_DIM] = value_grad


def norm_back(ctl, parts, windows, gain):
    tokens, width = parts.shape[1:]
    sources, rows, own, lanes = windows.shape
    last = lanes // LANES - 1
    return pl.pallas_call(
        norm_back_kernel,
        grid_spec=pltpu.PrefetchScalarGridSpec(
            num_scalar_prefetch=1,
            grid=(1,),
            in_specs=[
                whole(parts.shape),
                pl.BlockSpec(
                    (sources, rows, own, LANES), lambda i, ctl: (0, 0, 0, last * (1 - ctl[3]))
                ),
                whole(gain.shape),
            ],
            out_specs=whole((tokens, width)),
        ),
        out_shape=jax.ShapeDtypeStruct((tokens, width), BF16),
        compiler_params=params(1, SMALL_LIMIT),
        name="norm_back",
    )(ctl, parts, windows, gain)


def turn_kernel(ctl_ref, f_ref, out_ref):
    odd = ctl_ref[3]
    turned = f_ref[...].reshape(-1, f_ref.shape[-1]).T
    rows = out_ref.shape[0]
    spare = turned.shape[0] - rows

    @pl.when(odd == 0)
    def _():
        out_ref[...] = turned[:rows]

    @pl.when(odd != 0)
    def _():
        out_ref[...] = turned[spare:]


def turn(ctl, windows, feat):
    sources, rows, own, width = windows.shape
    tokens = sources * own
    return pl.pallas_call(
        turn_kernel,
        grid_spec=pltpu.PrefetchScalarGridSpec(
            num_scalar_prefetch=1,
            grid=(rows,),
            in_specs=[pl.BlockSpec((sources, 1, own, width), lambda r, ctl: (0, r, 0, 0))],
            out_specs=pl.BlockSpec((feat, tokens), lambda r, ctl: (0, r)),
        ),
        out_shape=jax.ShapeDtypeStruct((feat, rows * tokens), BF16),
        compiler_params=params(1, SMALL_LIMIT),
        name="turn",
    )(ctl, windows)


def weight_kernel(ctl_ref, f_ref, *refs):
    pieces, (out_ref, grads_ref) = refs[:-2], refs[-2:]
    tokens = pieces[0].shape[0]
    for away, piece in enumerate(pieces):
        source = lax.rem(ctl_ref[4] + len(pieces) - away, len(pieces))
        grads_ref[pl.ds(pl.multiple_of(source * tokens, tokens), tokens)] = piece[...]
    out_ref[...] = jnp.dot(f_ref[...], grads_ref[...], preferred_element_type=F32).astype(BF16)


def weight_grad(ctl, turned, pieces):
    feat, tokens = turned.shape
    width = pieces[0].shape[1]
    return pl.pallas_call(
        weight_kernel,
        grid_spec=pltpu.PrefetchScalarGridSpec(
            num_scalar_prefetch=1,
            grid=(1,),
            in_specs=[whole(turned.shape)] + [whole(piece.shape) for piece in pieces],
            out_specs=whole((feat, width)),
            scratch_shapes=[pltpu.VMEM((tokens, width), BF16)],
        ),
        out_shape=jax.ShapeDtypeStruct((feat, width), BF16),
        compiler_params=params(1, SMALL_LIMIT),
        cost_estimate=pl.CostEstimate(
            flops=2 * feat * tokens * width, bytes_accessed=2 * feat * tokens, transcendentals=0
        ),
        name="weight_grad",
    )(ctl, turned, *pieces)


def finish_kernel(parts_ref, key_ref, value_ref):
    total = jnp.sum(parts_ref[...].astype(F32), axis=0)
    for group in range(total.shape[1] // (2 * HEAD_DIM)):
        cols = slice(group * HEAD_DIM, (group + 1) * HEAD_DIM)
        at = 2 * group * HEAD_DIM
        key_ref[:, cols] = total[:, at : at + HEAD_DIM]
        value_ref[:, cols] = total[:, at + HEAD_DIM : at + 2 * HEAD_DIM]


def finish(parts):
    out = jax.ShapeDtypeStruct((parts.shape[1], parts.shape[2] // 2), F32)
    return pl.pallas_call(
        finish_kernel,
        out_shape=[out, out],
        compiler_params=params(0, SMALL_LIMIT),
        name="finish",
    )(parts)


def exchange(array, axes):
    return lax.all_to_all(array, axes, split_axis=0, concat_axis=0, tiled=True)


def on_device(queries, features, w_key, w_value, key_gain, out_grad, tile_counts, text_start):
    dp, seq = lax.axis_size("dp"), lax.axis_size("seq")
    rows, own, feat = features.shape
    text_dev = queries.shape[1]
    pairs = 2 * w_key.shape[1]
    tokens = rows * own
    gain = key_gain.reshape(1, HEAD_DIM)
    dp_index, seq_index = lax.axis_index("dp"), lax.axis_index("seq")
    ctl = jnp.stack(
        [tile_counts[0], seq_index * text_dev, text_start[0], dp_index & 1, dp_index]
    )
    feats = features.reshape(tokens, feat)
    send, key_pre = project(feats, w_key, w_value, gain, seq)
    windows = cut(feats, key_pre, dp)
    arrived = exchange(send.reshape(seq * dp, own, pairs), ("seq", "dp"))
    windows, arrived, ctl = lax.optimization_barrier((windows, arrived, ctl))
    keys_values = arrived.reshape(seq * tokens, pairs)
    windows = exchange(windows, "dp").reshape(dp, rows, own, -1)
    probs, score_grads, grads = attend(ctl, queries[0], out_grad[0], keys_values)
    grads, windows = lax.optimization_barrier((grads, windows))
    shares = exchange(grads.reshape(seq, tokens, pairs), "seq")
    attended = apply(ctl, probs, keys_values, text_dev, HEAD_DIM, True, "attended")
    shares, attended = lax.optimization_barrier((shares, attended))
    rounded = norm_back(ctl, shares, windows, gain)
    everywhere = [rounded]
    for away in range(1, dp):
        to = [(source, (source + away) % dp) for source in range(dp)]
        everywhere.append(lax.ppermute(rounded, "dp", to))
    turned = turn(ctl, windows, feat // dp)
    partial = weight_grad(ctl, turned, everywhere)
    pieces = exchange(partial.reshape(seq, feat // dp // seq, pairs), "seq")
    query_grad = apply(ctl, score_grads, keys_values, text_dev, 0, False, "query_grad")
    pieces, query_grad = lax.optimization_barrier((pieces, query_grad))
    key_weight, value_weight = finish(pieces)
    return attended[None], query_grad[None], key_weight, value_weight


def solution(mesh):
    placed = (
        P("dp", "seq", "mp"),
        P(None, ("seq", "dp"), None),
        P(None, "mp"),
        P(None, "mp"),
        P(),
        P("dp", "seq", "mp"),
        P("dp"),
        P("dp"),
    )
    return jax.shard_map(
        on_device,
        mesh=mesh,
        in_specs=placed,
        out_specs=(
            P("dp", "seq", "mp"),
            P("dp", "seq", "mp"),
            P(("dp", "seq"), "mp"),
            P(("dp", "seq"), "mp"),
        ),
        check_vma=False,
    )
```
